32 devices in a mesh: dp: 16 (over z, x, core), tensor: 2 (over y).
Axes of the slice: x: 2, y: 2, z: 4, core: 2. Of those that a mesh axis runs over, the one named last changes fastest.
Arguments:
- x_in: bfloat16 [16384, 1024], P(('dp', 'tensor')), may hold values from -6 to 6
- source: bfloat16 [16384, 1024], P(('dp', 'tensor')), may hold values from -6 to 6
- segment: int32 [16384], P(('dp', 'tensor')), may hold values from 0 to 12, as said below
- parent: int32 [16, 13], P('dp'), may hold values from 0 to 11, as said below
- norm_gain: bfloat16 [1024, 3], P('dp'), may hold values from 0.099609375 to 1.8984375
- norm_bias: bfloat16 [1024, 3], P('dp'), may hold values from -3 to 3
- self_query: bfloat16 [1024, 1024], P('dp', 'tensor'), may hold values from -0.1875 to 0.1875
- self_key: bfloat16 [1024, 1024], P('dp', 'tensor'), may hold values from -0.1875 to 0.1875
- self_value: bfloat16 [1024, 1024], P('dp', 'tensor'), may hold values from -0.1875 to 0.1875
- self_output: bfloat16 [1024, 1024], P('dp', 'tensor'), may hold values from -0.75 to 0.75
- cross_query: bfloat16 [1024, 1024], P('dp', 'tensor'), may hold values from -0.1875 to 0.1875
- cross_key: bfloat16 [1024, 1024], P('dp', 'tensor'), may hold values from -0.1875 to 0.1875
- cross_value: bfloat16 [1024, 1024], P('dp', 'tensor'), may hold values from -0.1875 to 0.1875
- cross_output: bfloat16 [1024, 1024], P('dp', 'tensor'), may hold values from -1 to 1
- ffn_up: bfloat16 [1024, 4096], P('dp', 'tensor'), may hold values from -0.1875 to 0.1875
- ffn_down: bfloat16 [1024, 4096], P('dp', 'tensor'), may hold values from -0.09375 to 0.09375
- cotangent: bfloat16 [16384, 1024], P(('dp', 'tensor')), may hold values from -6 to 6
Outputs:
- x_out: bfloat16 [16384, 1024], P(('dp', 'tensor'))
- x_grad: float32 [16384, 1024], P(('dp', 'tensor'))
- source_grad: float32 [16384, 1024], P(('dp', 'tensor'))
- norm_gain_grad: float32 [1024, 3], P('dp')
- norm_bias_grad: float32 [1024, 3], P('dp')
- self_query_grad: float32 [1024, 1024], P('dp', 'tensor')
- self_key_grad: float32 [1024, 1024], P('dp', 'tensor')
- self_value_grad: float32 [1024, 1024], P('dp', 'tensor')
- self_output_grad: float32 [1024, 1024], P('dp', 'tensor')
- cross_query_grad: float32 [1024, 1024], P('dp', 'tensor')
- cross_key_grad: float32 [1024, 1024], P('dp', 'tensor')
- cross_value_grad: float32 [1024, 1024], P('dp', 'tensor')
- cross_output_grad: float32 [1024, 1024], P('dp', 'tensor')
- ffn_up_grad: float32 [1024, 4096], P('dp', 'tensor')
- ffn_down_grad: float32 [1024, 4096], P('dp', 'tensor')
The draws below stay inside these ranges and needn't reach their ends.
Inputs may be any that keep to these rules, and one draw needn't show every extreme that they name: Within each tree, segment ids never fall along the tokens, start with the trunk 0 on more than half of the tree's 1024 tokens, and every id holds at least one token. parent[t, 0] = 0, parent[t, b] < b for every other segment b, and parent[t, 12] = 11 in every tree.
All inputs are finite; a program needn't handle non-finite values.
Results may differ from the reference program's by a relative error of at most 0.022.
Values may be sent and summed in bfloat16 or wider, within the bound.
No kernel may reach another device: no remote copies, remote signals or barrier semaphores. Data moves between devices by JAX's collectives and lax.ppermute only.
A program may use at most 192 MiB of HBM per device.

```python
import jax
import jax.numpy as jnp
from jax import lax

D = 1024
HEADS = 16
HEAD_DIM = 64
FF = 4096
NODES = 13
SRC_LEN = 1024
TREE = 1024
TREES = 16
TOKENS = 16384
SOURCES = 16384


def draw_segment(key, part):
    tree_count = TOKENS // TREE
    first_key = jax.random.fold_in(key, 1)
    second_key = jax.random.fold_in(key, 2)
    rest_count = jax.random.randint(first_key, (tree_count, 1), TREE // 4, TREE // 2)
    trunk_len = TREE - rest_count
    node_weights = jax.random.randint(second_key, (tree_count, NODES - 1), 1, 5)
    running = jnp.cumsum(node_weights, 1)
    counts = jnp.arange(1, NODES, dtype=jnp.int32)[None, :]
    node_ends = trunk_len + counts + (rest_count - (NODES - 1)) * running // running[:, -1:]
    node_starts = jnp.concatenate([trunk_len, node_ends[:, :-1]], 1)
    positions = jnp.arange(TREE, dtype=jnp.int32)
    labels = jnp.sum((positions[None, :, None] >= node_starts[:, None, :]).astype(jnp.int32), -1)
    return labels.reshape(TOKENS).astype(jnp.int32)


def draw_parent(key, part):
    tree_count = TOKENS // TREE
    node_ids = jnp.arange(NODES, dtype=jnp.int32)
    upper_bound = jnp.maximum(node_ids, 1)
    raw_draw = jax.random.randint(jax.random.fold_in(key, 3), (tree_count, NODES), 0, upper_bound[None, :])
    raw_draw = jnp.where(node_ids[None, :] == NODES - 1, NODES - 2, raw_draw)
    return jnp.where(node_ids[None, :] == 0, 0, raw_draw).astype(jnp.int32)


def strengthened(values, key, source, target, shards_of, factor):
    owner, partner = [(jnp.arange(values.shape[dim]) // (values.shape[dim] // shards_of)).reshape([-1 if axis == dim else 1 for axis in range(values.ndim)]) for dim in (source, target)]
    chosen = jax.random.permutation(key, shards_of)[partner]
    strong = (owner == chosen) | (owner == (partner + shards_of // 2) % shards_of)
    return jnp.where(strong, factor * values, values)


def level_of(stream_key, dims, split, low, top_value):
    factor_of = 1.0
    for position, shards_of in split:
        steps = jax.random.uniform(jax.random.fold_in(jax.random.fold_in(stream_key, 6), position), (shards_of,), jnp.float32, low / len(split), top_value / len(split))
        factor_of = factor_of * jnp.repeat(jnp.exp(steps), dims[position] // shards_of).reshape((-1,) + (1,) * (len(dims) - 1 - position))
    return factor_of


def scatter_about(stream_key, extent, spread, reach, shards=(), kind=jnp.bfloat16):
    entries = jax.random.normal(stream_key, extent, jnp.float32) * spread
    if len(shards) > 0:
        entries = level_of(stream_key, extent, shards, -0.22, 0.18) * entries
    return jnp.clip(entries, min=-reach, max=reach).astype(kind)


def heavy_noise(own_key, dims, deviation, most, cuts, heavy, kind=jnp.bfloat16):
    array = deviation * jax.random.normal(own_key, dims, jnp.float32)
    if cuts:
        array = array * level_of(own_key, dims, cuts, -0.22, 0.18)
    return jnp.clip(strengthened(array, jax.random.fold_in(own_key, 3), *heavy), -most, most).astype(kind)


def setup_inputs(seed: int = 0) -> dict:
    streams_of = jax.random.split(jax.random.key(seed), 18)
    x_in = scatter_about(streams_of[0], (TOKENS, D), 1.0, 6.0, ((0, 32),))
    source = scatter_about(streams_of[1], (SOURCES, D), 1.0, 6.0, ((0, 32),))
    segment = draw_segment(jax.random.fold_in(streams_of[17], 71), 0)
    parent = draw_parent(jax.random.fold_in(streams_of[17], 71), 0)
    norm_gain = jnp.clip(1.0 + 0.18 * jax.random.normal(streams_of[4], (D, 3), jnp.float32), 0.099609375, 1.8984375).astype(jnp.bfloat16)
    norm_bias = scatter_about(streams_of[5], (D, 3), 0.3, 3.0, ((0, 16),))
    self_query = scatter_about(streams_of[6], (D, D), D ** -0.5, 0.1875, ((0, 16), (1, 2)))
    self_key = scatter_about(streams_of[7], (D, D), D ** -0.5, 0.1875, ((0, 16), (1, 2)))
    self_value = scatter_about(streams_of[8], (D, D), D ** -0.5, 0.1875, ((0, 16), (1, 2)))
    self_output = scatter_about(streams_of[9], (D, D), (D // 16) ** -0.5, 0.75, ((0, 16), (1, 2)))
    cross_query = scatter_about(streams_of[10], (D, D), D ** -0.5, 0.1875, ((0, 16), (1, 2)))
    cross_key = scatter_about(streams_of[11], (D, D), D ** -0.5, 0.1875, ((0, 16), (1, 2)))
    cross_value = scatter_about(streams_of[12], (D, D), D ** -0.5, 0.1875, ((0, 16), (1, 2)))
    cross_output = scatter_about(streams_of[13], (D, D), (D // 32) ** -0.5, 1.0, ((0, 16), (1, 2)))
    ffn_up = scatter_about(streams_of[14], (D, FF), D ** -0.5, 0.1875, ((0, 16), (1, 2)))
    ffn_down = scatter_about(streams_of[15], (D, FF), FF ** -0.5, 0.09375, ((0, 16), (1, 2)))
    cotangent = heavy_noise(streams_of[16], (TOKENS, D), 1.0, 6.0, ((0, 32),), (0, 1, 32, 2.75))
    return {"x_in": x_in, "source": source, "segment": segment, "parent": parent, "norm_gain": norm_gain, "norm_bias": norm_bias, "self_query": self_query, "self_key": self_key, "self_value": self_value, "self_output": self_output, "cross_query": cross_query, "cross_key": cross_key, "cross_value": cross_value, "cross_output": cross_output, "ffn_up": ffn_up, "ffn_down": ffn_down, "cotangent": cotangent}


EPSILON = 1e-05
NEGATIVE = -1000000000.0

@jax.custom_vjp
def low(v):
    return lax.optimization_barrier(v.astype(jnp.bfloat16)).astype(jnp.float32)

@jax.custom_vjp
def low_back(v):
    return v

def low_keep(v):
    return (low(v), None)

def low_pass(kept, grad):
    return (grad,)

def back_keep(v):
    return (v, None)

def back_low(kept, grad):
    return (low(grad),)
low.defvjp(low_keep, low_pass)
low_back.defvjp(back_keep, back_low)

def rounded(values):
    return low(low_back(values))

def matmul(former, latter):
    return jnp.matmul(former, latter, precision=lax.Precision.HIGHEST)

def layer_norm(values, gain_row, offset):
    centered = values - lax.optimization_barrier(jnp.mean(values, -1, keepdims=True))
    variance = lax.optimization_barrier(jnp.mean(centered * centered, -1, keepdims=True))
    return centered * lax.rsqrt(variance + EPSILON) * gain_row + offset

def split_heads(values):
    return values.reshape(values.shape[0], HEADS, HEAD_DIM).transpose(1, 0, 2)

def attention(hidden, memory, query_w, key_w, value_w, output_w, visible):
    queries = split_heads(rounded(matmul(hidden, query_w)))
    key_rows = split_heads(rounded(matmul(memory, key_w)))
    value_rows = split_heads(rounded(matmul(memory, value_w)))
    scores = jnp.einsum('hqd,hkd->hqk', queries, key_rows, precision=lax.Precision.HIGHEST) * HEAD_DIM ** (-0.5)
    scores = low_back(scores)
    if visible is not None:
        scores = jnp.where(visible[None], scores, NEGATIVE)
    row_top = lax.optimization_barrier(jnp.max(scores, -1, keepdims=True))
    exponent = jnp.exp(scores - row_top)
    weights = low(exponent / lax.optimization_barrier(jnp.sum(exponent, -1, keepdims=True)))
    mixture = jnp.einsum('hqk,hkd->hqd', weights, value_rows, precision=lax.Precision.HIGHEST)
    mixture = rounded(mixture.transpose(1, 0, 2).reshape(hidden.shape[0], HEADS * HEAD_DIM))
    return low_back(matmul(mixture, output_w.T))

def decoder_block(residual, memory, visible, parameters):
    gain_cols, shift_cols, self_q, self_k, self_v, self_o, cross_q, cross_k, cross_v, cross_o, up_w, down_w = parameters
    normed = low(layer_norm(residual, gain_cols[:, 0], shift_cols[:, 0]))
    residual = residual + attention(normed, normed, self_q, self_k, self_v, self_o, visible)
    normed = low(layer_norm(residual, gain_cols[:, 1], shift_cols[:, 1]))
    residual = residual + attention(normed, memory, cross_q, cross_k, cross_v, cross_o, None)
    normed = low(layer_norm(residual, gain_cols[:, 2], shift_cols[:, 2]))
    activated = low(jax.nn.gelu(low_back(matmul(normed, up_w)), approximate=False))
    return residual + low_back(matmul(activated, down_w.T))

def tree_visible(segment_row, parent_row):
    node_ids = jnp.arange(NODES, dtype=jnp.int32)
    current = node_ids
    ancestor = jnp.zeros((NODES, NODES), dtype=bool)
    for depth_step in range(NODES):
        ancestor = ancestor | (node_ids[:, None] == current[None, :])
        current = parent_row[current]
    positions = jnp.arange(segment_row.shape[0], dtype=jnp.int32)
    return ancestor[segment_row[None, :], segment_row[:, None]] & (positions[None, :] <= positions[:, None])

def reference(x_in, source, segment, parent, norm_gain, norm_bias, self_query, self_key, self_value, self_output, cross_query, cross_key, cross_value, cross_output, ffn_up, ffn_down, cotangent):
    parameters = tuple((weight.astype(jnp.float32) for weight in (norm_gain, norm_bias, self_query, self_key, self_value, self_output, cross_query, cross_key, cross_value, cross_output, ffn_up, ffn_down)))
    residuals = x_in.astype(jnp.float32).reshape(TREES, TREE, D)
    memories = source.astype(jnp.float32).reshape(TREES, SRC_LEN, D)
    segments = segment.reshape(TREES, TREE)
    incomings = cotangent.astype(jnp.float32).reshape(TREES, TREE, D)

    def one_tree(totals, members):
        residual, memory, segment_row, parent_row, incoming = members
        visible = tree_visible(segment_row, parent_row)

        def forward(residual_in, memory_in, *weights):
            return decoder_block(residual_in, memory_in, visible, weights)
        result, backward = jax.vjp(forward, residual, memory, *parameters)
        gradients = backward(incoming)
        totals = tuple((total + gradient for total, gradient in zip(totals, gradients[2:])))
        return (totals, (result, gradients[0], gradients[1]))
    initial = tuple((jnp.zeros_like(weight) for weight in parameters))
    totals, outputs = lax.scan(one_tree, initial, (residuals, memories, segments, parent, incomings))
    results, input_grads, memory_grads = outputs
    return (results.reshape(TOKENS, D).astype(jnp.bfloat16), input_grads.reshape(TOKENS, D), memory_grads.reshape(SOURCES, D), totals[0], totals[1], totals[2], totals[3], totals[4], totals[5], totals[6], totals[7], totals[8], totals[9], totals[10], totals[11])
```

```python
import functools

import jax
import jax.numpy as jnp
import numpy as np
from jax import lax
from jax.experimental import pallas as pl
from jax.experimental.pallas import tpu as pltpu
from jax.sharding import PartitionSpec as P

HEAD_DIM = 64
PAIR = 128
EPSILON = 1e-05
HIDDEN = -1e30
AXES = ("dp", "tensor")
BF = jnp.bfloat16
F32 = jnp.float32
VMEM_LIMIT = 50 * 2**20


def dot(former, latter, dims, kind=F32):
    return lax.dot_general(former, latter, (dims, ((), ())), preferred_element_type=kind)


def mm(former, latter, kind=F32):
    return dot(former, latter, ((1,), (0,)), kind)


def mm_lt(former, latter, kind=F32):
    return dot(former, latter, ((0,), (0,)), kind)


def mm_rt(former, latter, kind=F32):
    return dot(former, latter, ((1,), (1,)), kind)


def head_masks(values):
    lane = lax.broadcasted_iota(jnp.int32, values.shape, 1)
    zero = jnp.zeros_like(values)
    return (
        jnp.where(lane < HEAD_DIM, values, zero),
        jnp.where(lane >= HEAD_DIM, values, zero),
    )


def causal_bias(rows, columns, row_start, column_start):
    row = lax.broadcasted_iota(jnp.int32, (rows, columns), 0) + row_start
    column = lax.broadcasted_iota(jnp.int32, (rows, columns), 1) + column_start
    return row, column


def attention_kernel(tree, block, *refs):
    if tree:
        q_ref, k_ref, v_ref, qbits_ref, kbits_ref, o_ref, lse_ref, bias_ref = refs
    else:
        q_ref, k_ref, v_ref, o_ref, lse_ref = refs
    tokens = q_ref.shape[0]
    keys = k_ref.shape[0]
    half = tokens // 2
    if tree:

        @pl.when(pl.program_id(0) == 0)
        def _():
            row, column = causal_bias(half, half, 0, 0)
            seen = (qbits_ref[half:, :] & kbits_ref[:, half:]) != 0
            bias_ref[...] = jnp.where(seen & (column <= row), 0.0, HIDDEN)

    lane = lax.broadcasted_iota(jnp.int32, (block, PAIR), 1)
    for start in range(0, tokens, block):
        last = start + block if tree else keys
        queries = head_masks(q_ref[start : start + block, :] * BF(HEAD_DIM ** (-0.5)))
        key_rows = k_ref[:last, :]
        value_rows = v_ref[:last, :]
        outs = []
        sums = []
        for side in range(2):
            scores = mm_rt(queries[side], key_rows)
            if tree:
                if start < half:
                    row, column = causal_bias(block, block, 0, 0)
                    tail = scores[:, start:] + jnp.where(column <= row, 0.0, HIDDEN)
                    split = start
                else:
                    tail = (
                        scores[:, half:]
                        + bias_ref[start - half : start - half + block, : last - half]
                    )
                    split = half
                scores = tail if split == 0 else jnp.concatenate([scores[:, :split], tail], 1)
            top = jnp.max(scores, 1, keepdims=True)
            weights = jnp.exp(scores - top)
            total = jnp.sum(weights, 1, keepdims=True)
            outs.append(mm(weights.astype(BF), value_rows) * (1.0 / total))
            sums.append(top + jnp.log(total))
        o_ref[start : start + block, :] = jnp.where(lane < HEAD_DIM, outs[0], outs[1]).astype(BF)
        lse_ref[start : start + block, :] = jnp.where(lane < HEAD_DIM, sums[0], sums[1])


def attention(q, k, v, offsets, pairs, bits, block=256):
    tokens = q.shape[0]
    tree = bits is not None

    def spec(rows, shift):
        return pl.BlockSpec((rows, PAIR), lambda i, shift=shift: (0, i + shift))

    in_specs = [spec(tokens, offsets[0]), spec(k.shape[0], offsets[1]), spec(v.shape[0], offsets[2])]
    operands = [q, k, v]
    scratch = []
    if tree:
        in_specs += [
            pl.BlockSpec((tokens, 1), lambda i: (0, 0)),
            pl.BlockSpec((1, tokens), lambda i: (0, 0)),
        ]
        operands += list(bits)
        scratch = [pltpu.VMEM((tokens // 2, tokens // 2), F32)]
    return pl.pallas_call(
        functools.partial(attention_kernel, tree, block),
        grid=(pairs,),
        in_specs=in_specs,
        out_specs=[spec(tokens, 0), spec(tokens, 0)],
        out_shape=[
            jax.ShapeDtypeStruct((tokens, pairs * PAIR), BF),
            jax.ShapeDtypeStruct((tokens, pairs * PAIR), F32),
        ],
        scratch_shapes=scratch,
        compiler_params=pltpu.CompilerParams(vmem_limit_bytes=VMEM_LIMIT),
        cost_estimate=pl.CostEstimate(
            flops=4 * tokens * k.shape[0] * PAIR * 2 * pairs,
            bytes_accessed=tokens * pairs * PAIR * 12,
            transcendentals=tokens * k.shape[0] * 2 * pairs,
        ),
    )(*operands)


def attention_back_kernel(tree, block, *refs):
    if tree:
        (q_ref, k_ref, v_ref, o_ref, lse_ref, do_ref, qbits_ref, kbits_ref,
         dq_ref, dk_ref, dv_ref, dq_acc, bias_ref) = refs
    else:
        q_ref, k_ref, v_ref, o_ref, lse_ref, do_ref, dq_ref, dk_ref, dv_ref, dq_acc = refs
    tokens = q_ref.shape[0]
    keys = k_ref.shape[0]
    half = tokens // 2
    scale = HEAD_DIM ** (-0.5)
    if tree:

        @pl.when(pl.program_id(0) == 0)
        def _():
            row, column = causal_bias(half, half, 0, 0)
            seen = (kbits_ref[half:, :] & qbits_ref[:, half:]) != 0
            bias_ref[...] = jnp.where(seen & (row <= column), 0.0, HIDDEN)

    queries = head_masks(q_ref[...] * BF(scale))
    grads = head_masks(do_ref[...])
    pick_row = lax.broadcasted_iota(jnp.int32, (8, PAIR), 0)
    pick_lane = lax.broadcasted_iota(jnp.int32, (8, PAIR), 1)
    pick = ((pick_lane // HEAD_DIM) == pick_row).astype(F32)
    product = do_ref[...].astype(F32) * o_ref[...].astype(F32)
    delta = lax.dot_general(
        pick, product, (((1,), (1,)), ((), ())), precision=lax.Precision.HIGHEST,
        preferred_element_type=F32,
    )
    lse_rows = jnp.transpose(lse_ref[...])
    for start in range(0, keys, block):
        first = start if tree else 0
        key_rows = k_ref[start : start + block, :]
        key_masked = head_masks(key_rows)
        value_rows = v_ref[start : start + block, :]
        dv = None
        dk = None
        dq = None
        for side in range(2):
            stat = lse_rows[side * HEAD_DIM : side * HEAD_DIM + 1, first:]
            scores = mm_rt(key_rows, queries[side][first:, :]) - stat
            if tree:
                if start < half:
                    row, column = causal_bias(block, block, 0, 0)
                    head = scores[:, :block] + jnp.where(row <= column, 0.0, HIDDEN)
                    scores = jnp.concatenate([head, scores[:, block:]], 1)
                else:
                    scores = scores + bias_ref[start - half : start - half + block, first - half :]
            weights = jnp.exp(scores)
            dv_part = mm(weights.astype(BF), grads[side][first:, :])
            weight_grad = mm_rt(value_rows, grads[side][first:, :])
            score_grad = (weights * (weight_grad - delta[side : side + 1, first:])).astype(BF)
            dk_part = mm(score_grad, queries[side][first:, :])
            dq_part = mm_lt(score_grad, key_masked[side])
            dv = dv_part if dv is None else dv + dv_part
            dk = dk_part if dk is None else dk + dk_part
            dq = dq_part if dq is None else dq + dq_part
        dv_ref[start : start + block, :] = dv.astype(BF)
        dk_ref[start : start + block, :] = dk.astype(BF)
        if start == 0:
            dq_acc[...] = dq
        else:
            dq_acc[first:, :] += dq
    dq_ref[...] = (dq_acc[...] * scale).astype(BF)


def attention_back(q, k, v, o, lse, do, offsets, pairs, bits, block=256):
    tokens = q.shape[0]
    keys = k.shape[0]
    tree = bits is not None

    def spec(rows, shift):
        return pl.BlockSpec((rows, PAIR), lambda i, shift=shift: (0, i + shift))

    in_specs = [
        spec(tokens, offsets[0]), spec(keys, offsets[1]), spec(keys, offsets[2]),
        spec(tokens, 0), spec(tokens, 0), spec(tokens, 0),
    ]
    operands = [q, k, v, o, lse, do]
    scratch = [pltpu.VMEM((tokens, PAIR), F32)]
    if tree:
        in_specs += [
            pl.BlockSpec((1, tokens), lambda i: (0, 0)),
            pl.BlockSpec((tokens, 1), lambda i: (0, 0)),
        ]
        operands += list(bits)
        scratch.append(pltpu.VMEM((tokens // 2, tokens // 2), F32))
    return pl.pallas_call(
        functools.partial(attention_back_kernel, tree, block),
        grid=(pairs,),
        in_specs=in_specs,
        out_specs=[spec(tokens, 0), spec(keys, 0), spec(keys, 0)],
        out_shape=[
            jax.ShapeDtypeStruct((tokens, pairs * PAIR), BF),
            jax.ShapeDtypeStruct((keys, pairs * PAIR), BF),
            jax.ShapeDtypeStruct((keys, pairs * PAIR), BF),
        ],
        scratch_shapes=scratch,
        compiler_params=pltpu.CompilerParams(vmem_limit_bytes=VMEM_LIMIT),
        cost_estimate=pl.CostEstimate(
            flops=10 * tokens * keys * PAIR * 2 * pairs,
            bytes_accessed=tokens * pairs * PAIR * 20,
            transcendentals=tokens * keys * 2 * pairs,
        ),
    )(*operands)


class Links:
    def __init__(self, dp_size):
        self.devices = 2 * dp_size
        self.places = dp_size // 2
        self.grid = dp_size == 16
        if self.grid:
            near = [[0, 1, 2, 3], [1, 0, 2, 3], [2, 3, 1, 0], [3, 2, 1, 0]]
            self.order = np.array(
                [
                    [2 * near[place // 2][pos % 4] + ((place % 2) ^ (pos // 4)) for pos in range(8)]
                    for place in range(8)
                ]
            )
        else:
            self.order = np.tile(np.arange(self.places), (self.places, 1))

    def send(self, values, pairs):
        return lax.ppermute(values, AXES, pairs)

    def quad(self, values, edges):
        pairs = [(4 * m + s, 4 * m + t) for m in range(self.places) for s, t in edges]
        return self.send(values, pairs)

    def swap_trees(self, values):
        return self.quad(values, [(0, 0), (1, 2), (2, 1), (3, 3)])

    def swap_cores(self, values):
        return self.quad(values, [(0, 2), (1, 3), (2, 0), (3, 1)])

    def side_first(self, values):
        return self.quad(values, [(0, 0), (1, 2), (2, 1), (3, 3)])

    def side_second(self, values):
        return self.quad(values, [(0, 1), (1, 3), (3, 2), (2, 0)])

    def side_second_back(self, values):
        return self.quad(values, [(1, 0), (3, 1), (2, 3), (0, 2)])

    def x_swap(self, values):
        return self.send(values, [(i, i ^ 4) for i in range(self.devices)])

    def z_pairs(self, edges):
        return [(8 * s + i, 8 * t + i) for s, t in edges for i in range(8)]

    def z_near(self, values):
        return self.send(values, self.z_pairs([(0, 1), (1, 0), (2, 3), (3, 2)]))

    def z_middle(self, values):
        return self.send(values, self.z_pairs([(1, 2), (2, 1)]))

    def z_out(self, values):
        return self.send(values, self.z_pairs([(1, 0), (2, 3)]))

    def z_in(self, values):
        return self.send(values, self.z_pairs([(0, 1), (3, 2)]))

    def gather_z(self, shard, inner):
        beside = self.z_near(shard)
        pair = jnp.concatenate([shard, beside], 0)
        middle = self.z_middle(pair)
        outer = self.z_out(middle)
        return jnp.concatenate([pair, jnp.where(inner, middle, outer)], 0)

    def groups(self):
        return [[2 * m + c for m in range(self.places)] for c in range(2)]

    def gather(self, shard, inner, side_last):
        if not self.grid:
            whole = lax.all_gather(shard, "dp", axis=0, tiled=True, axis_index_groups=self.groups())
            return self.side_first(whole), self.side_second(whole)
        column = self.gather_z(shard, inner)
        return self.gather_rest(column, side_last)

    def gather_rest(self, column, side_last):
        if side_last:
            whole = jnp.concatenate([column, self.x_swap(column)], 0)
            return self.side_first(whole), self.side_second(whole)
        former, latter = self.side_first(column), self.side_second(column)
        return (
            jnp.concatenate([former, self.x_swap(former)], 0),
            jnp.concatenate([latter, self.x_swap(latter)], 0),
        )

    def add(self, former, latter):
        return (former.astype(F32) + latter.astype(F32)).astype(BF)

    def scatter(self, former, latter, side_first):
        if not self.grid:
            both = self.side_first(former).astype(F32) + self.side_second_back(latter).astype(F32)
            return lax.psum_scatter(
                both, "dp", scatter_dimension=0, tiled=True, axis_index_groups=self.groups()
            )
        rows = former.shape[0] // 2
        if side_first:
            both = self.add(self.side_first(former), self.side_second_back(latter))
            column = self.add(both[:rows], self.x_swap(both[rows:]))
        else:
            former = self.add(former[:rows], self.x_swap(former[rows:]))
            latter = self.add(latter[:rows], self.x_swap(latter[rows:]))
            column = self.add(self.side_first(former), self.side_second_back(latter))
        near, far = column[: rows // 2], column[rows // 2 :]
        far = self.add(far, self.z_in(far))
        near = self.add(near, self.z_middle(far))
        block = rows // 4
        return near[:block].astype(F32) + self.z_near(near[block:]).astype(F32)

    def total(self, values):
        if not self.grid:
            return lax.psum(values, AXES)
        for bit in (2, 4, 8, 16, 1):
            values = values + self.send(values, [(i, i ^ bit) for i in range(self.devices)])
        return values


def ancestor_bits(segment_all, parent_row):
    nodes = parent_row.shape[0]
    node_ids = jnp.arange(nodes, dtype=jnp.int32)
    current = node_ids
    seen = jnp.zeros((nodes,), jnp.int32)
    for _ in range(nodes):
        seen = seen | jnp.left_shift(1, current)
        current = jnp.sum(jnp.where(current[:, None] == node_ids[None, :], parent_row[None, :], 0), 1)
    query_bits = jnp.sum(
        jnp.where(segment_all[:, None] == node_ids[None, :], seen[None, :], 0), 1
    )
    return query_bits, jnp.left_shift(1, segment_all)


def norm_stats(values):
    mean = jnp.mean(values, -1, keepdims=True)
    centered = values - mean
    variance = jnp.mean(centered * centered, -1, keepdims=True)
    return centered, lax.rsqrt(variance + EPSILON)


def norm(values, gain_row, offset):
    centered, inverse = norm_stats(values)
    return centered * inverse * gain_row + offset


def norm_back(values, gain_row, grad):
    centered, inverse = norm_stats(values)
    normed = centered * inverse
    scaled = grad * gain_row
    back = inverse * (
        scaled
        - jnp.mean(scaled, -1, keepdims=True)
        - normed * jnp.mean(scaled * normed, -1, keepdims=True)
    )
    return back, grad * normed


def shards(
    links,
    x_in,
    source,
    segment,
    parent,
    norm_gain,
    norm_bias,
    self_query,
    self_key,
    self_value,
    self_output,
    cross_query,
    cross_key,
    cross_value,
    cross_output,
    ffn_up,
    ffn_down,
    cotangent,
):
    half, width = x_in.shape
    tokens = 2 * half
    rows = self_query.shape[0]
    heads_width = self_query.shape[1]
    hidden = ffn_up.shape[1]
    pairs = heads_width // PAIR
    place = lax.axis_index("dp") // 2
    core = lax.axis_index("dp") % 2
    first_core = core == 0

    inner = None
    if links.grid:
        height = place // 2
        inner = (height == 1) | (height == 2)

    index = np.arange(width)
    part, position, lowest = index // (width // 2), index % (width // 2) // rows, index % rows
    table = np.stack(
        [
            np.stack([order[position] * 2 * rows + (part ^ side) * rows + lowest for side in range(2)])
            for order in links.order
        ]
    ).astype(np.int32)
    wanted = jnp.asarray(table)[place, core]
    reorder = (jnp.arange(width, dtype=jnp.int32)[:, None] == wanted[None, :]).astype(BF)

    def both_halves(mine):
        other = links.swap_cores(mine)
        return jnp.concatenate(
            [jnp.where(first_core, mine, other), jnp.where(first_core, other, mine)], 0
        )

    def my_half(values):
        return jnp.where(first_core, values[:half], values[half:])

    def other_half(values):
        return jnp.where(first_core, values[half:], values[:half])

    def take_in(values):
        return both_halves(links.swap_trees(mm(values, reorder, BF)))

    def hand_out(values, kind):
        return mm_rt(links.swap_trees(values.astype(BF)), reorder, kind)

    pad = PAIR - norm_gain.shape[1] - norm_bias.shape[1]
    norms_shard = jnp.concatenate(
        [norm_gain, norm_bias, jnp.zeros((rows, pad), BF)], 1
    )
    self_shard = jnp.concatenate([self_query, self_key, self_value, self_output, norms_shard], 1)
    cross_shard = jnp.concatenate([cross_query, cross_key, cross_value, cross_output], 1)
    self_halves = links.gather(self_shard, inner, True)
    cross_halves = links.gather(cross_shard, inner, False)
    up_halves = links.gather(ffn_up, inner, True)
    down_halves = links.gather(ffn_down, inner, False)

    def columns(halves, start, stop):
        return jnp.concatenate([halves[0][:, start:stop], halves[1][:, start:stop]], 0)

    three = 3 * heads_width
    four = 4 * heads_width
    self_qkv = columns(self_halves, 0, three)
    self_o = columns(self_halves, three, four)
    norms = columns(self_halves, four, four + 8).astype(F32).T
    cross_q = columns(cross_halves, 0, heads_width)
    cross_kv = columns(cross_halves, heads_width, three)
    cross_o = columns(cross_halves, three, four)
    up_w = jnp.concatenate(up_halves, 0)
    down_w = jnp.concatenate(down_halves, 0)
    gain = [norms[i : i + 1] for i in range(3)]
    shift = [norms[i + 3 : i + 4] for i in range(3)]

    x_zero = take_in(x_in).astype(F32)
    source_all = take_in(source)
    nodes = parent.shape[1]
    labels = jnp.concatenate(
        [segment, parent[0], jnp.zeros((PAIR - nodes,), jnp.int32)]
    ).reshape(-1, PAIR)
    labels = links.swap_trees(labels)
    segment_rows = half // PAIR
    segment_all = both_halves(labels[:segment_rows]).reshape(tokens)
    query_bits, key_bits = ancestor_bits(segment_all, labels[segment_rows, :nodes])
    forward_bits = (query_bits[:, None], key_bits[None, :])
    backward_bits = (query_bits[None, :], key_bits[:, None])
    grad_top = take_in(cotangent)

    def joined(part):
        return part.astype(F32) + links.swap_cores(part).astype(F32)

    def joined_half(part):
        return my_half(part).astype(F32) + links.swap_cores(other_half(part)).astype(F32)

    hidden_one = norm(x_zero, gain[0], shift[0]).astype(BF)
    qkv = mm(hidden_one, self_qkv, BF)
    self_places = (0, pairs, 2 * pairs)
    mixed_one, lse_one = attention(qkv, qkv, qkv, self_places, pairs, forward_bits)
    x_one = x_zero + joined(mm_rt(mixed_one, self_o, BF))
    hidden_two = norm(x_one, gain[1], shift[1]).astype(BF)
    cross_queries = mm(hidden_two, cross_q, BF)
    memory = mm(source_all, cross_kv, BF)
    cross_places = (0, 0, pairs)
    mixed_two, lse_two = attention(cross_queries, memory, memory, cross_places, pairs, None)
    x_two = x_one + joined(mm_rt(mixed_two, cross_o, BF))
    hidden_three = norm(x_two, gain[2], shift[2]).astype(BF)
    active = mm(hidden_three, up_w)
    normal = 0.5 * (1.0 + lax.erf(active * np.float32(0.5**0.5)))
    slope = (
        normal + active * jnp.exp(-0.5 * active * active) * np.float32((2.0 * np.pi) ** -0.5)
    ).astype(BF)
    activated = (active * normal).astype(BF)
    x_three = my_half(x_two) + joined_half(mm_rt(activated, down_w, BF))
    x_out = hand_out(x_three, BF)

    def grad_halves(former, latter):
        middle = width // 2
        return mm_lt(former[:, :middle], latter, BF), mm_lt(former[:, middle:], latter, BF)

    down_grad = links.scatter(*grad_halves(grad_top, activated), False)
    active_grad = (mm(grad_top, down_w) * slope.astype(F32)).astype(BF)
    up_grad = links.scatter(*grad_halves(hidden_three, active_grad), True)
    normed_grad = joined(mm_rt(active_grad, up_w, BF))

    def norm_sums(values, grad):
        return jnp.sum(my_half(values), 0), jnp.sum(my_half(grad), 0)

    back, gain_part = norm_back(x_two, gain[2], normed_grad)
    gain_three, shift_three = norm_sums(gain_part, normed_grad)
    grad_two = grad_top.astype(F32) + back
    grad_two_low = grad_two.astype(BF)

    mixed_grad = mm(grad_two_low, cross_o, BF)
    dq, dk, dv = attention_back(
        cross_queries, memory, memory, mixed_two, lse_two, mixed_grad, cross_places, pairs, None
    )
    dkv = jnp.concatenate([dk, dv], 1)
    cross_q_grad = grad_halves(hidden_two, dq)
    cross_kv_grad = grad_halves(source_all, dkv)
    cross_o_grad = grad_halves(grad_two_low, mixed_two)
    cross_grad = links.scatter(
        jnp.concatenate([cross_q_grad[0], cross_kv_grad[0], cross_o_grad[0]], 1),
        jnp.concatenate([cross_q_grad[1], cross_kv_grad[1], cross_o_grad[1]], 1),
        False,
    )
    normed_grad = joined(mm_rt(dq, cross_q, BF))
    source_grad = hand_out(joined_half(mm_rt(dkv, cross_kv, BF)), F32)
    back, gain_part = norm_back(x_one, gain[1], normed_grad)
    gain_two, shift_two = norm_sums(gain_part, normed_grad)
    grad_one = grad_two + back
    grad_one_low = grad_one.astype(BF)

    mixed_grad = mm(grad_one_low, self_o, BF)
    dq, dk, dv = attention_back(
        qkv, qkv, qkv, mixed_one, lse_one, mixed_grad, self_places, pairs, backward_bits
    )
    dqkv = jnp.concatenate([dq, dk, dv], 1)
    self_o_grad = grad_halves(grad_one_low, mixed_one)
    self_qkv_grad = grad_halves(hidden_one, dqkv)
    self_grad = links.scatter(
        jnp.concatenate([self_qkv_grad[0], self_o_grad[0]], 1),
        jnp.concatenate([self_qkv_grad[1], self_o_grad[1]], 1),
        True,
    )
    normed_grad = joined_half(mm_rt(dqkv, self_qkv, BF))
    back, gain_part = norm_back(my_half(x_zero), gain[0], normed_grad)
    gain_one, shift_one = jnp.sum(gain_part, 0), jnp.sum(normed_grad, 0)
    x_grad = hand_out(my_half(grad_one) + back, F32)

    side = lax.axis_index("tensor")
    held = jnp.asarray(table)[place, side]
    stacked = jnp.stack(
        [gain_one, gain_two, gain_three, shift_one, shift_two, shift_three,
         jnp.zeros_like(gain_one), jnp.zeros_like(gain_one)]
    )
    plain = lax.dot_general(
        stacked,
        (jnp.arange(width, dtype=jnp.int32)[None, :] == held[:, None]).astype(F32),
        (((1,), (0,)), ((), ())),
        precision=lax.Precision.HIGHEST,
        preferred_element_type=F32,
    )
    norm_total = links.total(plain)
    norm_mine = lax.dynamic_slice(norm_total, (0, lax.axis_index("dp") * rows), (8, rows)).T

    def piece(values, number):
        return values[:, number * heads_width : (number + 1) * heads_width]

    return (
        x_out,
        x_grad,
        source_grad,
        norm_mine[:, :3],
        norm_mine[:, 3:6],
        piece(self_grad, 0),
        piece(self_grad, 1),
        piece(self_grad, 2),
        piece(self_grad, 3),
        piece(cross_grad, 0),
        piece(cross_grad, 1),
        piece(cross_grad, 2),
        piece(cross_grad, 3),
        up_grad,
        down_grad,
    )


def solution(mesh):
    rows = P(AXES, None)
    split = P("dp", "tensor")
    narrow = P("dp", None)
    placed = (rows, rows, P(AXES), narrow, narrow, narrow) + (split,) * 10 + (rows,)
    return jax.shard_map(
        functools.partial(shards, Links(mesh.shape["dp"])),
        mesh=mesh,
        in_specs=placed,
        out_specs=(rows, rows, rows, narrow, narrow) + (split,) * 10,
        check_vma=False,
    )
```

```python
import functools

import jax
import jax.numpy as jnp
import numpy as np
from jax import lax
from jax.experimental import pallas as pl
from jax.experimental.pallas import tpu as pltpu
from jax.sharding import PartitionSpec as P

HEAD_DIM = 64
PAIR = 128
EPSILON = 1e-05
HIDDEN = -1e30
AXES = ("dp", "tensor")
BF = jnp.bfloat16
F32 = jnp.float32
VMEM_LIMIT = 50 * 2**20
KERNEL_COST = pl.CostEstimate(flops=1, bytes_accessed=1024, transcendentals=0)


def dot(former, latter, dims, kind=F32):
    return lax.dot_general(former, latter, (dims, ((), ())), preferred_element_type=kind)


def mm(former, latter, kind=F32):
    return dot(former, latter, ((1,), (0,)), kind)


def mm_lt(former, latter, kind=F32):
    return dot(former, latter, ((0,), (0,)), kind)


def mm_rt(former, latter, kind=F32):
    return dot(former, latter, ((1,), (1,)), kind)


def head_masks(values):
    lane = lax.broadcasted_iota(jnp.int32, values.shape, 1)
    zero = jnp.zeros_like(values)
    return (
        jnp.where(lane < HEAD_DIM, values, zero),
        jnp.where(lane >= HEAD_DIM, values, zero),
    )


def causal_bias(rows, columns, row_start, column_start):
    row = lax.broadcasted_iota(jnp.int32, (rows, columns), 0) + row_start
    column = lax.broadcasted_iota(jnp.int32, (rows, columns), 1) + column_start
    return row, column


def attention_kernel(tree, block, *refs):
    if tree:
        q_ref, k_ref, v_ref, qbits_ref, kbits_ref, o_ref, lse_ref, bias_ref = refs
    else:
        q_ref, k_ref, v_ref, o_ref, lse_ref = refs
    tokens = q_ref.shape[0]
    keys = k_ref.shape[0]
    half = tokens // 2
    if tree:

        @pl.when(pl.program_id(0) == 0)
        def _():
            row, column = causal_bias(half, half, 0, 0)
            seen = (qbits_ref[half:, :] & kbits_ref[:, half:]) != 0
            bias_ref[...] = jnp.where(seen & (column <= row), 0.0, HIDDEN)

    lane = lax.broadcasted_iota(jnp.int32, (block, PAIR), 1)
    for start in range(0, tokens, block):
        last = start + block if tree else keys
        queries = head_masks(q_ref[start : start + block, :] * BF(HEAD_DIM ** (-0.5)))
        key_rows = k_ref[:last, :]
        value_rows = v_ref[:last, :]
        outs = []
        sums = []
        for side in range(2):
            scores = mm_rt(queries[side], key_rows)
            if tree:
                if start < half:
                    row, column = causal_bias(block, block, 0, 0)
                    tail = scores[:, start:] + jnp.where(column <= row, 0.0, HIDDEN)
                    split = start
                else:
                    tail = (
                        scores[:, half:]
                        + bias_ref[start - half : start - half + block, : last - half]
                    )
                    split = half
                scores = tail if split == 0 else jnp.concatenate([scores[:, :split], tail], 1)
            top = jnp.max(scores, 1, keepdims=True)
            weights = jnp.exp(scores - top)
            total = jnp.sum(weights, 1, keepdims=True)
            outs.append(mm(weights.astype(BF), value_rows) * (1.0 / total))
            sums.append(top + jnp.log(total))
        o_ref[start : start + block, :] = jnp.where(lane < HEAD_DIM, outs[0], outs[1]).astype(BF)
        lse_ref[start : start + block, :] = jnp.where(lane < HEAD_DIM, sums[0], sums[1])


def attention(q, k, v, offsets, pairs, bits, block=256):
    tokens = q.shape[0]
    tree = bits is not None

    def spec(rows, shift):
        return pl.BlockSpec((rows, PAIR), lambda i, shift=shift: (0, i + shift))

    in_specs = [spec(tokens, offsets[0]), spec(k.shape[0], offsets[1]), spec(v.shape[0], offsets[2])]
    operands = [q, k, v]
    scratch = []
    if tree:
        in_specs += [
            pl.BlockSpec((tokens, 1), lambda i: (0, 0)),
            pl.BlockSpec((1, tokens), lambda i: (0, 0)),
        ]
        operands += list(bits)
        scratch = [pltpu.VMEM((tokens // 2, tokens // 2), F32)]
    return pl.pallas_call(
        functools.partial(attention_kernel, tree, block),
        grid=(pairs,),
        in_specs=in_specs,
        out_specs=[spec(tokens, 0), spec(tokens, 0)],
        out_shape=[
            jax.ShapeDtypeStruct((tokens, pairs * PAIR), BF),
            jax.ShapeDtypeStruct((tokens, pairs * PAIR), F32),
        ],
        scratch_shapes=scratch,
        compiler_params=pltpu.CompilerParams(vmem_limit_bytes=VMEM_LIMIT),
        cost_estimate=KERNEL_COST,
    )(*operands)


def attention_back_kernel(tree, block, *refs):
    if tree:
        (q_ref, k_ref, v_ref, o_ref, lse_ref, do_ref, qbits_ref, kbits_ref,
         dq_ref, dk_ref, dv_ref, dq_acc, bias_ref) = refs
    else:
        q_ref, k_ref, v_ref, o_ref, lse_ref, do_ref, dq_ref, dk_ref, dv_ref, dq_acc = refs
    tokens = q_ref.shape[0]
    keys = k_ref.shape[0]
    half = tokens // 2
    scale = HEAD_DIM ** (-0.5)
    if tree:

        @pl.when(pl.program_id(0) == 0)
        def _():
            row, column = causal_bias(half, half, 0, 0)
            seen = (kbits_ref[half:, :] & qbits_ref[:, half:]) != 0
            bias_ref[...] = jnp.where(seen & (row <= column), 0.0, HIDDEN)

    queries = head_masks(q_ref[...] * BF(scale))
    grads = head_masks(do_ref[...])
    pick_row = lax.broadcasted_iota(jnp.int32, (8, PAIR), 0)
    pick_lane = lax.broadcasted_iota(jnp.int32, (8, PAIR), 1)
    pick = ((pick_lane // HEAD_DIM) == pick_row).astype(F32)
    product = do_ref[...].astype(F32) * o_ref[...].astype(F32)
    delta = lax.dot_general(
        pick, product, (((1,), (1,)), ((), ())), precision=lax.Precision.HIGHEST,
        preferred_element_type=F32,
    )
    lse_rows = jnp.transpose(lse_ref[...])
    for start in range(0, keys, block):
        first = start if tree else 0
        key_rows = k_ref[start : start + block, :]
        key_masked = head_masks(key_rows)
        value_rows = v_ref[start : start + block, :]
        dv = None
        dk = None
        dq = None
        for side in range(2):
            stat = lse_rows[side * HEAD_DIM : side * HEAD_DIM + 1, first:]
            scores = mm_rt(key_rows, queries[side][first:, :]) - stat
            if tree:
                if start < half:
                    row, column = causal_bias(block, block, 0, 0)
                    head = scores[:, :block] + jnp.where(row <= column, 0.0, HIDDEN)
                    scores = jnp.concatenate([head, scores[:, block:]], 1)
                else:
                    scores = scores + bias_ref[start - half : start - half + block, first - half :]
            weights = jnp.exp(scores)
            dv_part = mm(weights.astype(BF), grads[side][first:, :])
            weight_grad = mm_rt(value_rows, grads[side][first:, :])
            score_grad = (weights * (weight_grad - delta[side : side + 1, first:])).astype(BF)
            dk_part = mm(score_grad, queries[side][first:, :])
            dq_part = mm_lt(score_grad, key_masked[side])
            dv = dv_part if dv is None else dv + dv_part
            dk = dk_part if dk is None else dk + dk_part
            dq = dq_part if dq is None else dq + dq_part
        dv_ref[start : start + block, :] = dv.astype(BF)
        dk_ref[start : start + block, :] = dk.astype(BF)
        if start == 0:
            dq_acc[...] = dq
        else:
            dq_acc[first:, :] += dq
    dq_ref[...] = (dq_acc[...] * scale).astype(BF)


def attention_back(q, k, v, o, lse, do, offsets, pairs, bits, block=256):
    tokens = q.shape[0]
    keys = k.shape[0]
    tree = bits is not None

    def spec(rows, shift):
        return pl.BlockSpec((rows, PAIR), lambda i, shift=shift: (0, i + shift))

    in_specs = [
        spec(tokens, offsets[0]), spec(keys, offsets[1]), spec(keys, offsets[2]),
        spec(tokens, 0), spec(tokens, 0), spec(tokens, 0),
    ]
    operands = [q, k, v, o, lse, do]
    scratch = [pltpu.VMEM((tokens, PAIR), F32)]
    if tree:
        in_specs += [
            pl.BlockSpec((1, tokens), lambda i: (0, 0)),
            pl.BlockSpec((tokens, 1), lambda i: (0, 0)),
        ]
        operands += list(bits)
        scratch.append(pltpu.VMEM((tokens // 2, tokens // 2), F32))
    return pl.pallas_call(
        functools.partial(attention_back_kernel, tree, block),
        grid=(pairs,),
        in_specs=in_specs,
        out_specs=[spec(tokens, 0), spec(keys, 0), spec(keys, 0)],
        out_shape=[
            jax.ShapeDtypeStruct((tokens, pairs * PAIR), BF),
            jax.ShapeDtypeStruct((keys, pairs * PAIR), BF),
            jax.ShapeDtypeStruct((keys, pairs * PAIR), BF),
        ],
        scratch_shapes=scratch,
        compiler_params=pltpu.CompilerParams(vmem_limit_bytes=VMEM_LIMIT),
        cost_estimate=KERNEL_COST,
    )(*operands)


class Links:
    def __init__(self, dp_size):
        self.devices = 2 * dp_size
        self.places = dp_size // 2
        self.grid = dp_size == 16

    def begin(self):
        self.place = lax.axis_index("dp") // 2
        self.core = lax.axis_index("dp") % 2
        self.side = lax.axis_index("tensor")
        self.home = self.core == self.side

    def send(self, values, pairs):
        return lax.ppermute(values, AXES, pairs)

    def quad(self, values, edges):
        pairs = [(4 * m + s, 4 * m + t) for m in range(self.places) for s, t in edges]
        return self.send(values, pairs)

    def cross_begin(self, values):
        return values, self.quad(values, [(1, 2), (2, 1)])

    def cross_end(self, pending):
        return jnp.where(self.home, *pending)

    def cross(self, values):
        return self.cross_end(self.cross_begin(values))

    def swap_cores(self, values):
        return self.quad(values, [(0, 2), (1, 3), (2, 0), (3, 1)])

    def gather(self, shard):
        return lax.all_gather(shard, "dp", axis=0, tiled=True)

    def sides_begin(self, shard):
        return self.cross_begin(shard), self.quad(shard, [(0, 1), (1, 3), (3, 2), (2, 0)])

    def gather_sides_first(self, pending):
        former, latter = self.cross_end(pending[0]), pending[1]
        first_side = self.side == 0
        both = jnp.concatenate(
            [jnp.where(first_side, former, latter), jnp.where(first_side, latter, former)], 0
        )
        groups = [[2 * m + c for m in range(self.places)] for c in range(2)]
        return lax.all_gather(both, "dp", axis=0, tiled=True, axis_index_groups=groups)

    def scatter(self, crossed):
        return lax.psum_scatter(crossed, "dp", scatter_dimension=0, tiled=True).astype(F32)

    def total(self, values, bits):
        if not self.grid:
            return lax.psum(values, AXES) if 1 in bits else values
        for bit in bits:
            values = values + self.send(values, [(i, i ^ bit) for i in range(self.devices)])
        return values


def pick(values, index, axis):
    return lax.dynamic_index_in_dim(values, index, axis, keepdims=False)


def rounded_sum(former, latter):
    return (former.astype(F32) + latter.astype(F32)).astype(BF)


def together(*values):
    return lax.optimization_barrier(values)


class Scatter:
    def __init__(self, links, first, second):
        self.links = links
        self.state = first, second

    def exchange(self, values, axis, bit, index):
        kept, sent = pick(values, index, axis), pick(values, 1 - index, axis)
        return kept, self.links.send(sent, [(i, i ^ bit) for i in range(self.links.devices)])

    def sides(self, values, axis):
        links = self.links
        former, latter = pick(values, links.side, axis), pick(values, 1 - links.side, axis)
        return links.cross_begin(former), links.quad(latter, [(1, 0), (3, 1), (2, 3), (0, 2)])

    def sides_end(self, pending):
        return rounded_sum(self.links.cross_end(pending[0]), pending[1])

    def first(self):
        links = self.links
        if not links.grid:
            whole = jnp.concatenate(self.state, 1)
            self.state = links.scatter(links.cross(whole))
            return
        former, latter = (
            part.reshape(2, 2, 2, 2, part.shape[0] // 16, part.shape[1]) for part in self.state
        )
        self.state = self.sides(former, 3), self.exchange(latter, 2, 4, links.place % 2)

    def second(self):
        links = self.links
        if links.grid:
            former, latter = self.sides_end(self.state[0]), rounded_sum(*self.state[1])
            self.state = self.exchange(former, 2, 4, links.place % 2), self.sides(latter, 2)

    def far(self):
        if self.links.grid:
            both = jnp.concatenate(
                [rounded_sum(*self.state[0]), self.sides_end(self.state[1])], -1
            )
            self.state = self.exchange(both, 0, 16, self.links.place // 4)

    def near(self):
        if self.links.grid:
            whole = rounded_sum(*self.state)
            self.state = self.exchange(whole, 0, 8, self.links.place // 2 % 2)

    def result(self):
        if self.links.grid:
            self.state = self.state[0].astype(F32) + self.state[1].astype(F32)
        return self.state

    def after(self, *values):
        self.state, values = lax.optimization_barrier((self.state, values))
        return values


def ancestor_bits(segment_all, parent_row):
    nodes = parent_row.shape[0]
    node_ids = jnp.arange(nodes, dtype=jnp.int32)
    current = node_ids
    seen = jnp.zeros((nodes,), jnp.int32)
    for _ in range(nodes):
        seen = seen | jnp.left_shift(1, current)
        current = jnp.sum(jnp.where(current[:, None] == node_ids[None, :], parent_row[None, :], 0), 1)
    query_bits = jnp.sum(
        jnp.where(segment_all[:, None] == node_ids[None, :], seen[None, :], 0), 1
    )
    return query_bits, jnp.left_shift(1, segment_all)


def norm_stats(values):
    mean = jnp.mean(values, -1, keepdims=True)
    centered = values - mean
    variance = jnp.mean(centered * centered, -1, keepdims=True)
    return centered, lax.rsqrt(variance + EPSILON)


def norm(values, gain_row, offset):
    centered, inverse = norm_stats(values)
    return centered * inverse * gain_row + offset


def norm_back(values, gain_row, grad):
    centered, inverse = norm_stats(values)
    normed = centered * inverse
    scaled = grad * gain_row
    back = inverse * (
        scaled
        - jnp.mean(scaled, -1, keepdims=True)
        - normed * jnp.mean(scaled * normed, -1, keepdims=True)
    )
    return back, grad * normed


def shards(
    links,
    x_in,
    source,
    segment,
    parent,
    norm_gain,
    norm_bias,
    self_query,
    self_key,
    self_value,
    self_output,
    cross_query,
    cross_key,
    cross_value,
    cross_output,
    ffn_up,
    ffn_down,
    cotangent,
):
    half, width = x_in.shape
    tokens = 2 * half
    rows = self_query.shape[0]
    heads_width = self_query.shape[1]
    hidden = ffn_up.shape[1]
    pairs = heads_width // PAIR
    links.begin()
    first_core = links.core == 0

    def both_halves(mine):
        other = links.swap_cores(mine)
        return jnp.concatenate(
            [jnp.where(first_core, mine, other), jnp.where(first_core, other, mine)], 0
        )

    def my_half(values):
        return jnp.where(first_core, values[:half], values[half:])

    def other_half(values):
        return jnp.where(first_core, values[half:], values[:half])

    def joined(part):
        return part.astype(F32) + links.swap_cores(part).astype(F32)

    def joined_half(part):
        return my_half(part).astype(F32) + links.swap_cores(other_half(part)).astype(F32)

    nodes = parent.shape[1]
    labels = jnp.concatenate(
        [segment, parent[0], jnp.zeros((PAIR - nodes,), jnp.int32)]
    ).reshape(-1, PAIR)
    segment_rows = half // PAIR
    pad = PAIR - norm_gain.shape[1] - norm_bias.shape[1]
    norms_shard = jnp.concatenate(
        [norm_gain, norm_bias, jnp.zeros((rows, pad), BF)], 1
    )
    two, three, four = 2 * heads_width, 3 * heads_width, 4 * heads_width
    self_w = links.gather(
        jnp.concatenate([self_query, self_key, self_value, self_output, norms_shard], 1)
    )
    cross_w = links.gather(
        jnp.concatenate([cross_query, cross_key, cross_value, cross_output], 1)
    )
    up_w = links.gather(ffn_up)
    moved = links.cross_begin(labels), links.cross_begin(x_in)
    others = links.cross_begin(jnp.concatenate([source, cotangent], 0))
    down_w = links.sides_begin(ffn_down)
    self_w, moved, others, down_w = together(self_w, moved, others, down_w)
    down_w = links.gather_sides_first(down_w)
    self_w = links.cross_begin(self_w)
    labels, x_mine = links.cross_end(moved[0]), links.cross_end(moved[1])
    others = links.cross_end(others)
    x_zero = both_halves(x_mine).astype(F32)
    segment_all = both_halves(labels[:segment_rows]).reshape(tokens)
    query_bits, key_bits = ancestor_bits(segment_all, labels[segment_rows, :nodes])
    forward_bits = (query_bits[:, None], key_bits[None, :])
    backward_bits = (query_bits[None, :], key_bits[:, None])
    source_all = both_halves(others[:half])
    grad_top = both_halves(others[half:])
    centered, inverse = norm_stats(x_zero)
    normed = centered * inverse
    self_w, normed, source_all, grad_top = together(self_w, normed, source_all, grad_top)
    self_w = links.cross_end(self_w)
    norms = self_w[:, four : four + 8].astype(F32).T
    gain = [norms[i : i + 1] for i in range(3)]
    shift = [norms[i + 3 : i + 4] for i in range(3)]

    hidden_one = (normed * gain[0] + shift[0]).astype(BF)
    hidden_one, cross_w = together(hidden_one, cross_w)
    cross_w = links.cross_begin(cross_w)
    qkv = mm(hidden_one, self_w[:, :three], BF)
    self_places = (0, pairs, 2 * pairs)
    mixed_one, lse_one = attention(qkv, qkv, qkv, self_places, pairs, forward_bits)
    x_one = x_zero + joined(mm_rt(mixed_one, self_w[:, three:four], BF))
    hidden_two = norm(x_one, gain[1], shift[1]).astype(BF)
    hidden_two, up_w = together(hidden_two, up_w)
    up_w = links.cross_begin(up_w)
    cross_w = links.cross_end(cross_w)
    cross_queries = mm(hidden_two, cross_w[:, :heads_width], BF)
    memory = mm(source_all, cross_w[:, heads_width:three], BF)
    cross_places = (0, 0, pairs)
    mixed_two, lse_two = attention(cross_queries, memory, memory, cross_places, pairs, None)
    x_two = x_one + joined(mm_rt(mixed_two, cross_w[:, three:four], BF))
    hidden_three = norm(x_two, gain[2], shift[2]).astype(BF)
    hidden_three, up_w = together(hidden_three, up_w)
    up_w = links.cross_end(up_w)
    active = mm(hidden_three, up_w)
    normal = 0.5 * (1.0 + lax.erf(active * np.float32(0.5**0.5)))
    slope = (
        normal + active * jnp.exp(-0.5 * active * active) * np.float32((2.0 * np.pi) ** -0.5)
    ).astype(BF)
    activated = (active * normal).astype(BF)
    down_grad = mm_lt(grad_top, activated, BF)
    down_w, down_grad, activated, slope = together(down_w, down_grad, activated, slope)

    def norm_sums(values, grad):
        return jnp.sum(my_half(values), 0), jnp.sum(my_half(grad), 0)

    down_grad = links.cross_begin(down_grad)
    active_grad = (mm(grad_top, down_w) * slope.astype(F32)).astype(BF)
    up_grad = links.cross_begin(mm_lt(hidden_three, active_grad, BF))
    out_part = mm_rt(activated, down_w, BF)
    normed_grad = joined(mm_rt(active_grad, up_w, BF))
    back, gain_part = norm_back(x_two, gain[2], normed_grad)
    gain_three, shift_three = norm_sums(gain_part, normed_grad)
    grad_two = grad_top.astype(F32) + back
    grad_two_low = grad_two.astype(BF)
    mixed_grad = mm(grad_two_low, cross_w[:, three:four], BF)
    dq, dk, dv = attention_back(
        cross_queries, memory, memory, mixed_two, lse_two, mixed_grad, cross_places, pairs, None
    )
    dq, dk, dv, down_grad = together(dq, dk, dv, down_grad)
    down_grad = links.scatter(links.cross_end(down_grad))
    part = mm_rt(dq, cross_w[:, :heads_width], BF)
    normed_grad = joined(part)
    dkv = jnp.concatenate([dk, dv], 1)
    cross_grad = Scatter(
        links,
        jnp.concatenate([mm_lt(hidden_two, dq, BF), mm_lt(grad_two_low, mixed_two, BF)], 1),
        mm_lt(source_all, dkv, BF),
    )
    cross_grad.first()
    back, gain_part = norm_back(x_one, gain[1], normed_grad)
    gain_two, shift_two = norm_sums(gain_part, normed_grad)
    grad_one = grad_two + back
    grad_one_low = grad_one.astype(BF)
    mixed_grad = mm(grad_one_low, self_w[:, three:four], BF)
    mixed_grad, up_grad = cross_grad.after(mixed_grad, up_grad)
    cross_grad.second()
    up_grad = links.scatter(links.cross_end(up_grad))
    x_three = (my_half(x_two) + joined_half(out_part)).astype(BF)
    source_part = joined_half(mm_rt(dkv, cross_w[:, heads_width:three], BF)).astype(BF)
    outs = links.cross_begin(jnp.concatenate([x_three, source_part], 0))
    dq, dk, dv = attention_back(
        qkv, qkv, qkv, mixed_one, lse_one, mixed_grad, self_places, pairs, backward_bits
    )
    dq, dk, dv = cross_grad.after(dq, dk, dv)
    cross_grad.far()
    dqkv = jnp.concatenate([dq, dk, dv], 1)
    qkv_grad = mm_lt(hidden_one, dqkv, BF)
    self_grad = Scatter(
        links,
        qkv_grad[:, :two],
        jnp.concatenate([qkv_grad[:, two:], mm_lt(grad_one_low, mixed_one, BF)], 1),
    )
    self_grad.first()
    normed_grad = joined_half(mm_rt(dqkv, self_w[:, :three], BF))
    back, gain_part = norm_back(my_half(x_zero), gain[0], normed_grad)
    gain_one, shift_one = jnp.sum(gain_part, 0), jnp.sum(normed_grad, 0)
    x_grad_mine = (my_half(grad_one) + back).astype(BF)
    sums = jnp.stack(
        [gain_one, gain_two, gain_three, shift_one, shift_two, shift_three,
         jnp.zeros_like(gain_one), jnp.zeros_like(gain_one)]
    )
    sums = links.total(sums, (2, 8))
    x_grad_mine, sums = self_grad.after(x_grad_mine, sums)
    self_grad.second()
    cross_grad.near()
    sums = links.total(sums, (16,))
    outs, sums, cross_grad.state = self_grad.after(outs, sums, cross_grad.state)
    self_grad.far()
    cross_grad = cross_grad.result()
    x_grad = links.cross_begin(x_grad_mine)
    sums = links.total(sums, (4, 1))
    outs = links.cross_end(outs)
    x_out = outs[:half]
    source_grad = outs[half:].astype(F32)
    x_grad, sums, cross_grad, x_out, source_grad = self_grad.after(
        x_grad, sums, cross_grad, x_out, source_grad
    )
    self_grad.near()
    x_grad = links.cross_end(x_grad).astype(F32)
    norm_mine = lax.dynamic_slice(sums, (0, lax.axis_index("dp") * rows), (8, rows)).T
    self_grad = self_grad.result()

    def piece(values, number):
        return values[:, number * heads_width : (number + 1) * heads_width]

    return (
        x_out,
        x_grad,
        source_grad,
        norm_mine[:, :3],
        norm_mine[:, 3:6],
        piece(self_grad, 0),
        piece(self_grad, 1),
        piece(self_grad, 2),
        piece(self_grad, 3),
        piece(cross_grad, 0),
        piece(cross_grad, 2),
        piece(cross_grad, 3),
        piece(cross_grad, 1),
        up_grad,
        down_grad,
    )


def solution(mesh):
    rows = P(AXES, None)
    split = P("dp", "tensor")
    narrow = P("dp", None)
    placed = (rows, rows, P(AXES), narrow, narrow, narrow) + (split,) * 10 + (rows,)
    return jax.shard_map(
        functools.partial(shards, Links(mesh.shape["dp"])),
        mesh=mesh,
        in_specs=placed,
        out_specs=(rows, rows, rows, narrow, narrow) + (split,) * 10,
        check_vma=False,
    )
```

```python
import functools

import jax
import jax.numpy as jnp
import numpy as np
from jax import lax
from jax.experimental import pallas as pl
from jax.experimental.pallas import tpu as pltpu
from jax.sharding import PartitionSpec as P

HEAD_DIM = 64
PAIR = 128
EPSILON = 1e-05
HIDDEN = -1e30
AXES = ("dp", "tensor")
BF = jnp.bfloat16
F32 = jnp.float32
VMEM_LIMIT = 50 * 2**20
KERNEL_COST = pl.CostEstimate(flops=1, bytes_accessed=1024, transcendentals=0)


def dot(former, latter, dims, kind=F32):
    return lax.dot_general(former, latter, (dims, ((), ())), preferred_element_type=kind)


def mm(former, latter, kind=F32):
    return dot(former, latter, ((1,), (0,)), kind)


def mm_lt(former, latter, kind=F32):
    return dot(former, latter, ((0,), (0,)), kind)


def mm_rt(former, latter, kind=F32):
    return dot(former, latter, ((1,), (1,)), kind)


def head_masks(values):
    lane = lax.broadcasted_iota(jnp.int32, values.shape, 1)
    zero = jnp.zeros_like(values)
    return (
        jnp.where(lane < HEAD_DIM, values, zero),
        jnp.where(lane >= HEAD_DIM, values, zero),
    )


def causal_bias(rows, columns, row_start, column_start):
    row = lax.broadcasted_iota(jnp.int32, (rows, columns), 0) + row_start
    column = lax.broadcasted_iota(jnp.int32, (rows, columns), 1) + column_start
    return row, column


def attention_kernel(tree, block, *refs):
    if tree:
        q_ref, k_ref, v_ref, qbits_ref, kbits_ref, o_ref, lse_ref, bias_ref = refs
    else:
        q_ref, k_ref, v_ref, o_ref, lse_ref = refs
    tokens = q_ref.shape[0]
    keys = k_ref.shape[0]
    half = tokens // 2
    if tree:

        @pl.when(pl.program_id(0) == 0)
        def _():
            row, column = causal_bias(half, half, 0, 0)
            seen = (qbits_ref[half:, :] & kbits_ref[:, half:]) != 0
            bias_ref[...] = jnp.where(seen & (column <= row), 0.0, HIDDEN)

    lane = lax.broadcasted_iota(jnp.int32, (block, PAIR), 1)
    for start in range(0, tokens, block):
        last = start + block if tree else keys
        queries = head_masks(q_ref[start : start + block, :] * BF(HEAD_DIM ** (-0.5)))
        key_rows = k_ref[:last, :]
        value_rows = v_ref[:last, :]
        outs = []
        sums = []
        for side in range(2):
            scores = mm_rt(queries[side], key_rows)
            if tree:
                if start < half:
                    row, column = causal_bias(block, block, 0, 0)
                    tail = scores[:, start:] + jnp.where(column <= row, 0.0, HIDDEN)
                    split = start
                else:
                    tail = (
                        scores[:, half:]
                        + bias_ref[start - half : start - half + block, : last - half]
                    )
                    split = half
                scores = tail if split == 0 else jnp.concatenate([scores[:, :split], tail], 1)
            top = jnp.max(scores, 1, keepdims=True)
            weights = jnp.exp(scores - top)
            total = jnp.sum(weights, 1, keepdims=True)
            outs.append(mm(weights.astype(BF), value_rows) * (1.0 / total))
            sums.append(top + jnp.log(total))
        o_ref[start : start + block, :] = jnp.where(lane < HEAD_DIM, outs[0], outs[1]).astype(BF)
        lse_ref[start : start + block, :] = jnp.where(lane < HEAD_DIM, sums[0], sums[1])


def attention(q, k, v, offsets, pairs, bits, block=256):
    tokens = q.shape[0]
    tree = bits is not None

    def spec(rows, shift):
        return pl.BlockSpec((rows, PAIR), lambda i, shift=shift: (0, i + shift))

    in_specs = [spec(tokens, offsets[0]), spec(k.shape[0], offsets[1]), spec(v.shape[0], offsets[2])]
    operands = [q, k, v]
    scratch = []
    if tree:
        in_specs += [
            pl.BlockSpec((tokens, 1), lambda i: (0, 0)),
            pl.BlockSpec((1, tokens), lambda i: (0, 0)),
        ]
        operands += list(bits)
        scratch = [pltpu.VMEM((tokens // 2, tokens // 2), F32)]
    return pl.pallas_call(
        functools.partial(attention_kernel, tree, block),
        grid=(pairs,),
        in_specs=in_specs,
        out_specs=[spec(tokens, 0), spec(tokens, 0)],
        out_shape=[
            jax.ShapeDtypeStruct((tokens, pairs * PAIR), BF),
            jax.ShapeDtypeStruct((tokens, pairs * PAIR), F32),
        ],
        scratch_shapes=scratch,
        compiler_params=pltpu.CompilerParams(vmem_limit_bytes=VMEM_LIMIT),
        cost_estimate=KERNEL_COST,
    )(*operands)


def attention_back_kernel(tree, block, *refs):
    if tree:
        (q_ref, k_ref, v_ref, o_ref, lse_ref, do_ref, qbits_ref, kbits_ref,
         dq_ref, dk_ref, dv_ref, dq_acc, bias_ref) = refs
    else:
        q_ref, k_ref, v_ref, o_ref, lse_ref, do_ref, dq_ref, dk_ref, dv_ref, dq_acc = refs
    tokens = q_ref.shape[0]
    keys = k_ref.shape[0]
    half = tokens // 2
    scale = HEAD_DIM ** (-0.5)
    if tree:

        @pl.when(pl.program_id(0) == 0)
        def _():
            row, column = causal_bias(half, half, 0, 0)
            seen = (kbits_ref[half:, :] & qbits_ref[:, half:]) != 0
            bias_ref[...] = jnp.where(seen & (row <= column), 0.0, HIDDEN)

    queries = head_masks(q_ref[...] * BF(scale))
    grads = head_masks(do_ref[...])
    pick_row = lax.broadcasted_iota(jnp.int32, (8, PAIR), 0)
    pick_lane = lax.broadcasted_iota(jnp.int32, (8, PAIR), 1)
    pick = ((pick_lane // HEAD_DIM) == pick_row).astype(F32)
    product = do_ref[...].astype(F32) * o_ref[...].astype(F32)
    delta = lax.dot_general(
        pick, product, (((1,), (1,)), ((), ())), precision=lax.Precision.HIGHEST,
        preferred_element_type=F32,
    )
    lse_rows = jnp.transpose(lse_ref[...])
    for start in range(0, keys, block):
        first = start if tree else 0
        key_rows = k_ref[start : start + block, :]
        key_masked = head_masks(key_rows)
        value_rows = v_ref[start : start + block, :]
        dv = None
        dk = None
        dq = None
        for side in range(2):
            stat = lse_rows[side * HEAD_DIM : side * HEAD_DIM + 1, first:]
            scores = mm_rt(key_rows, queries[side][first:, :]) - stat
            if tree:
                if start < half:
                    row, column = causal_bias(block, block, 0, 0)
                    head = scores[:, :block] + jnp.where(row <= column, 0.0, HIDDEN)
                    scores = jnp.concatenate([head, scores[:, block:]], 1)
                else:
                    scores = scores + bias_ref[start - half : start - half + block, first - half :]
            weights = jnp.exp(scores)
            dv_part = mm(weights.astype(BF), grads[side][first:, :])
            weight_grad = mm_rt(value_rows, grads[side][first:, :])
            score_grad = (weights * (weight_grad - delta[side : side + 1, first:])).astype(BF)
            dk_part = mm(score_grad, queries[side][first:, :])
            dq_part = mm_lt(score_grad, key_masked[side])
            dv = dv_part if dv is None else dv + dv_part
            dk = dk_part if dk is None else dk + dk_part
            dq = dq_part if dq is None else dq + dq_part
        dv_ref[start : start + block, :] = dv.astype(BF)
        dk_ref[start : start + block, :] = dk.astype(BF)
        if start == 0:
            dq_acc[...] = dq
        else:
            dq_acc[first:, :] += dq
    dq_ref[...] = (dq_acc[...] * scale).astype(BF)


def attention_back(q, k, v, o, lse, do, offsets, pairs, bits, block=256):
    tokens = q.shape[0]
    keys = k.shape[0]
    tree = bits is not None

    def spec(rows, shift):
        return pl.BlockSpec((rows, PAIR), lambda i, shift=shift: (0, i + shift))

    in_specs = [
        spec(tokens, offsets[0]), spec(keys, offsets[1]), spec(keys, offsets[2]),
        spec(tokens, 0), spec(tokens, 0), spec(tokens, 0),
    ]
    operands = [q, k, v, o, lse, do]
    scratch = [pltpu.VMEM((tokens, PAIR), F32)]
    if tree:
        in_specs += [
            pl.BlockSpec((1, tokens), lambda i: (0, 0)),
            pl.BlockSpec((tokens, 1), lambda i: (0, 0)),
        ]
        operands += list(bits)
        scratch.append(pltpu.VMEM((tokens // 2, tokens // 2), F32))
    return pl.pallas_call(
        functools.partial(attention_back_kernel, tree, block),
        grid=(pairs,),
        in_specs=in_specs,
        out_specs=[spec(tokens, 0), spec(keys, 0), spec(keys, 0)],
        out_shape=[
            jax.ShapeDtypeStruct((tokens, pairs * PAIR), BF),
            jax.ShapeDtypeStruct((keys, pairs * PAIR), BF),
            jax.ShapeDtypeStruct((keys, pairs * PAIR), BF),
        ],
        scratch_shapes=scratch,
        compiler_params=pltpu.CompilerParams(vmem_limit_bytes=VMEM_LIMIT),
        cost_estimate=KERNEL_COST,
    )(*operands)


def pick(values, index, axis):
    return lax.dynamic_index_in_dim(values, index, axis, keepdims=False)


class Pending:
    def __init__(self, finish, *received):
        self.finish, self.received = finish, list(received)

    def end(self):
        return self.finish(*self.received)


def wait(pendings, *values, computed=()):
    marks = [lax.slice(v, (0,) * v.ndim, (1,) * (v.ndim - 2) + (8, PAIR)) for v in computed]
    received, values, _ = lax.optimization_barrier(([p.received for p in pendings], values, marks))
    for pending, got in zip(pendings, received):
        pending.received = got
    return values


class Links:
    def __init__(self, dp_size):
        self.devices = 2 * dp_size
        self.places = dp_size // 2
        self.grid = dp_size == 16

    def begin(self):
        self.place = lax.axis_index("dp") // 2
        self.core = lax.axis_index("dp") % 2
        self.side = lax.axis_index("tensor")
        self.home = self.core == self.side

    def send(self, values, pairs):
        return lax.ppermute(values, AXES, pairs)

    def flip(self, values, bit):
        return self.send(values, [(i, i ^ bit) for i in range(self.devices)])

    def quad(self, values, edges):
        pairs = [(4 * m + s, 4 * m + t) for m in range(self.places) for s, t in edges]
        return self.send(values, pairs)

    def cross(self, values):
        return Pending(
            lambda got: jnp.where(self.home, values, got), self.quad(values, [(1, 2), (2, 1)])
        )

    def swap_cores(self, values):
        return self.quad(values, [(0, 2), (1, 3), (2, 0), (3, 1)])

    def groups(self):
        return [[2 * m + c for m in range(self.places)] for c in range(2)]

    def gather(self, shard):
        return lax.all_gather(shard, "dp", axis=0, tiled=True)

    def sides(self, shard):
        def finish(near, far):
            near = jnp.where(self.home, shard, near)
            first = self.side == 0
            return jnp.concatenate([jnp.where(first, near, far), jnp.where(first, far, near)], 0)

        return Pending(
            finish,
            self.quad(shard, [(1, 2), (2, 1)]),
            self.quad(shard, [(0, 1), (1, 3), (3, 2), (2, 0)]),
        )

    def gather_places(self, both):
        return lax.all_gather(both, "dp", axis=0, tiled=True, axis_index_groups=self.groups())

    def scatter(self, grad):
        return lax.psum_scatter(grad, "dp", scatter_dimension=0, tiled=True)

    def scatter_places(self, grad):
        return lax.psum_scatter(
            grad, "dp", scatter_dimension=0, tiled=True, axis_index_groups=self.groups()
        )

    def sides_back(self, parts, axis):
        mine, other = (
            jnp.concatenate([pick(part, index, axis) for part in parts], -1)
            for index in (self.side, 1 - self.side)
        )
        return Pending(
            lambda near, far: jnp.where(self.home, mine, near).astype(F32) + far.astype(F32),
            self.quad(mine, [(1, 2), (2, 1)]),
            self.quad(other, [(1, 0), (3, 1), (2, 3), (0, 2)]),
        )

    def halve(self, parts, axis, bit, index):
        kept, sent = (
            jnp.concatenate([pick(part, i, axis) for part in parts], -1) for i in (index, 1 - index)
        )
        return Pending(
            lambda got: kept.astype(F32) + got.astype(F32), self.flip(sent, bit)
        )

    def total(self, values, bits):
        if not self.grid:
            return lax.psum(values, AXES) if 1 in bits else values
        for bit in bits:
            values = values + self.flip(values, bit)
        return values


class Scatter:
    def __init__(self, links, first, second):
        self.links = links
        if not links.grid:
            whole = links.scatter_places(jnp.concatenate(list(first) + list(second), 1))
            self.state = [links.sides_back([whole.reshape(2, -1, whole.shape[1])], 0)]
            return
        former, latter = (
            [part.reshape(2, 2, 2, 2, part.shape[0] // 16, part.shape[1]) for part in parts]
            for parts in (first, second)
        )
        self.state = [
            links.sides_back(former, 3), links.halve(latter, 2, 4, links.place % 2)
        ]

    def second(self):
        links = self.links
        if links.grid:
            former, latter = (pending.end().astype(BF) for pending in self.state)
            self.state = [
                links.halve([former], 2, 4, links.place % 2), links.sides_back([latter], 2)
            ]

    def far(self):
        links = self.links
        if links.grid:
            both = jnp.concatenate([pending.end().astype(BF) for pending in self.state], -1)
            self.state = [links.halve([both], 0, 16, links.place // 4)]

    def near(self):
        links = self.links
        if links.grid:
            whole = self.state[0].end().astype(BF)
            self.state = [links.halve([whole], 0, 8, links.place // 2 % 2)]

    def result(self):
        return self.state[0].end()


def ancestor_bits(segment_all, parent_row):
    nodes = parent_row.shape[0]
    node_ids = jnp.arange(nodes, dtype=jnp.int32)
    current = node_ids
    seen = jnp.zeros((nodes,), jnp.int32)
    for _ in range(nodes):
        seen = seen | jnp.left_shift(1, current)
        current = jnp.sum(jnp.where(current[:, None] == node_ids[None, :], parent_row[None, :], 0), 1)
    query_bits = jnp.sum(
        jnp.where(segment_all[:, None] == node_ids[None, :], seen[None, :], 0), 1
    )
    return query_bits, jnp.left_shift(1, segment_all)


def norm_stats(values):
    mean = jnp.mean(values, -1, keepdims=True)
    centered = values - mean
    variance = jnp.mean(centered * centered, -1, keepdims=True)
    return centered, lax.rsqrt(variance + EPSILON)


def norm(values, gain_row, offset):
    centered, inverse = norm_stats(values)
    return centered * inverse * gain_row + offset


def norm_back(values, gain_row, grad):
    centered, inverse = norm_stats(values)
    normed = centered * inverse
    scaled = grad * gain_row
    back = inverse * (
        scaled
        - jnp.mean(scaled, -1, keepdims=True)
        - normed * jnp.mean(scaled * normed, -1, keepdims=True)
    )
    return back, grad * normed


def shards(
    links,
    x_in,
    source,
    segment,
    parent,
    norm_gain,
    norm_bias,
    self_query,
    self_key,
    self_value,
    self_output,
    cross_query,
    cross_key,
    cross_value,
    cross_output,
    ffn_up,
    ffn_down,
    cotangent,
):
    half, width = x_in.shape
    tokens = 2 * half
    rows = self_query.shape[0]
    heads_width = self_query.shape[1]
    hidden = ffn_up.shape[1]
    pairs = heads_width // PAIR
    links.begin()
    first_core = links.core == 0

    def both_halves(mine):
        other = links.swap_cores(mine)
        return jnp.concatenate(
            [jnp.where(first_core, mine, other), jnp.where(first_core, other, mine)], 0
        )

    def my_half(values, first=first_core):
        return jnp.where(first, values[:half], values[half:])

    def other_half(values, first=first_core):
        return jnp.where(first, values[half:], values[:half])

    def joined(part):
        return part.astype(F32) + links.swap_cores(part).astype(F32)

    def joined_half(part, first=first_core):
        sent = links.swap_cores(other_half(part, first))
        return my_half(part, first).astype(F32) + sent.astype(F32)

    nodes = parent.shape[1]
    labels = jnp.concatenate(
        [segment, parent[0], jnp.zeros((PAIR - nodes,), jnp.int32)]
    ).reshape(-1, PAIR)
    segment_rows = half // PAIR
    pad = PAIR - norm_gain.shape[1] - norm_bias.shape[1]
    norms_shard = jnp.concatenate(
        [norm_gain, norm_bias, jnp.zeros((rows, pad), BF)], 1
    )
    two, three, four = 2 * heads_width, 3 * heads_width, 4 * heads_width
    self_w = links.gather(
        jnp.concatenate([self_query, self_key, self_value, self_output, norms_shard], 1)
    )
    cross_w = links.gather(
        jnp.concatenate([cross_query, cross_key, cross_value, cross_output], 1)
    )
    up_w = links.gather(ffn_up)
    moved = [links.cross(x_in), links.cross(labels), links.cross(jnp.concatenate([source, cotangent], 0))]
    down_w = links.sides(ffn_down)
    whole = Pending(lambda got: got, self_w)
    wait(moved + [down_w, whole])
    self_w = links.cross(whole.end())
    down_w = links.gather_places(down_w.end())
    x_mine, labels, others = (pending.end() for pending in moved)
    x_zero = both_halves(x_mine).astype(F32)
    segment_all = both_halves(labels[:segment_rows]).reshape(tokens)
    query_bits, key_bits = ancestor_bits(segment_all, labels[segment_rows, :nodes])
    forward_bits = (query_bits[:, None], key_bits[None, :])
    backward_bits = (query_bits[None, :], key_bits[:, None])
    source_all = both_halves(others[:half])
    grad_top = both_halves(others[half:])
    centered, inverse = norm_stats(x_zero)
    normed = centered * inverse
    whole = Pending(lambda got: got, cross_w)
    wait([self_w, whole], computed=(normed, source_all, grad_top))
    cross_w = links.cross(whole.end())
    self_w = self_w.end()
    norms = self_w[:, four : four + 8].astype(F32).T
    gain = [norms[i : i + 1] for i in range(3)]
    shift = [norms[i + 3 : i + 4] for i in range(3)]

    hidden_one = (normed * gain[0] + shift[0]).astype(BF)
    qkv = mm(hidden_one, self_w[:, :three], BF)
    self_places = (0, pairs, 2 * pairs)
    mixed_one, lse_one = attention(qkv, qkv, qkv, self_places, pairs, forward_bits)
    x_one = x_zero + joined(mm_rt(mixed_one, self_w[:, three:four], BF))
    hidden_two = norm(x_one, gain[1], shift[1]).astype(BF)
    whole = Pending(lambda got: got, up_w)
    (hidden_two,) = wait([whole], hidden_two)
    up_w = links.cross(whole.end())
    cross_w = cross_w.end()
    cross_queries = mm(hidden_two, cross_w[:, :heads_width], BF)
    memory = mm(source_all, cross_w[:, heads_width:three], BF)
    cross_places = (0, 0, pairs)
    mixed_two, lse_two = attention(cross_queries, memory, memory, cross_places, pairs, None)
    x_two = x_one + joined(mm_rt(mixed_two, cross_w[:, three:four], BF))
    hidden_three = norm(x_two, gain[2], shift[2]).astype(BF)
    (hidden_three,) = wait([up_w], hidden_three)
    up_w = up_w.end()
    active = mm(hidden_three, up_w)
    normal = 0.5 * (1.0 + lax.erf(active * np.float32(0.5**0.5)))
    slope = (
        normal + active * jnp.exp(-0.5 * active * active) * np.float32((2.0 * np.pi) ** -0.5)
    ).astype(BF)
    activated = (active * normal).astype(BF)
    down_grad = mm_lt(grad_top, activated, BF)
    whole = Pending(lambda got: got, down_w)
    down_grad, activated, slope = wait([whole], down_grad, activated, slope)
    down_w = whole.end()

    def norm_sums(values, grad):
        return jnp.sum(my_half(values), 0), jnp.sum(my_half(grad), 0)

    down_grad = links.scatter_places(down_grad)
    active_grad = (mm(grad_top, down_w) * slope.astype(F32)).astype(BF)
    up_grad = links.cross(mm_lt(hidden_three, active_grad, BF))
    normed_grad = joined(mm_rt(active_grad, up_w, BF))
    back, gain_part = norm_back(x_two, gain[2], normed_grad)
    gain_three, shift_three = norm_sums(gain_part, normed_grad)
    grad_two = grad_top.astype(F32) + back
    grad_two_low = grad_two.astype(BF)
    mixed_grad = mm(grad_two_low, cross_w[:, three:four], BF)
    dq, dk, dv = attention_back(
        cross_queries, memory, memory, mixed_two, lse_two, mixed_grad, cross_places, pairs, None
    )
    down_grad = Pending(lambda got: got, down_grad)
    part = mm_rt(dq, cross_w[:, :heads_width], BF)
    dkv = jnp.concatenate([dk, dv], 1)
    cross_q_grad = mm_lt(hidden_two, dq, BF)
    cross_o_grad = mm_lt(grad_two_low, mixed_two, BF)
    cross_kv_grad = mm_lt(source_all, dkv, BF)
    normed_grad = joined(part)
    (gain_row,) = wait([up_grad, down_grad], gain[1], computed=(part, cross_q_grad, cross_o_grad))
    up_grad, gain_row = wait([], up_grad.end(), gain_row)
    up_grad = Pending(lambda got: got, links.scatter(up_grad))
    back, gain_part = norm_back(x_one, gain_row, normed_grad)
    gain_two, shift_two = norm_sums(gain_part, normed_grad)
    grad_one = grad_two + back
    grad_one_low = grad_one.astype(BF)
    self_o_grad = mm_lt(grad_one_low, mixed_one, BF)
    cross_grad = Scatter(
        links,
        [cross_q_grad, cross_o_grad, self_o_grad[:, : heads_width // 2]],
        [cross_kv_grad, self_o_grad[:, heads_width // 2 :]],
    )
    mixed_grad = mm(grad_one_low, self_w[:, three:four], BF)
    dq, dk, dv = attention_back(
        qkv, qkv, qkv, mixed_one, lse_one, mixed_grad, self_places, pairs, backward_bits
    )
    dqkv = jnp.concatenate([dq, dk, dv], 1)
    qkv_grad = mm_lt(hidden_one, dqkv, BF)
    self_grad = links.cross(qkv_grad)
    part = mm_rt(dqkv, self_w[:, :three], BF)
    part, down_late, cross_late = wait(
        cross_grad.state, part, down_w, cross_w, computed=(qkv_grad,)
    )
    cross_grad.second()
    normed_grad = joined_half(part)
    out_part = mm_rt(activated, down_late, BF)
    source_part = mm_rt(dkv, cross_late[:, heads_width:three], BF)
    wait([self_grad], computed=(out_part, source_part))
    self_grad, first_late, gain_zero = wait([], self_grad.end(), first_core, gain[0])
    self_grad = links.scatter(self_grad)
    x_three = (my_half(x_two, first_late) + joined_half(out_part, first_late)).astype(BF)
    source_part = joined_half(source_part, first_late).astype(BF)
    outs = [links.cross(v) for v in (x_three, source_part)]
    (gain_zero,) = wait(cross_grad.state, gain_zero)
    cross_grad.far()
    back, gain_part = norm_back(my_half(x_zero), gain_zero, normed_grad)
    gain_one, shift_one = jnp.sum(gain_part, 0), jnp.sum(normed_grad, 0)
    x_grad_mine = (my_half(grad_one) + back).astype(BF)
    sums = jnp.stack(
        [gain_one, gain_two, gain_three, shift_one, shift_two, shift_three,
         jnp.zeros_like(gain_one), jnp.zeros_like(gain_one)]
    )
    (sums,) = wait(outs, sums, computed=(x_grad_mine,))
    outs.append(links.cross(x_grad_mine))
    down_grad = links.sides_back([down_grad.end().reshape(2, -1, hidden)], 0)
    x_out, source_grad = (pending.end() for pending in outs[:2])
    source_grad = source_grad.astype(F32)
    up_grad = up_grad.end().astype(F32)
    sums = links.total(sums, (2, 4))
    (sums,) = wait(cross_grad.state + [down_grad], sums, computed=(source_grad, up_grad))
    cross_grad.near()
    down_grad = down_grad.end()
    sums = links.total(sums, (8, 16, 1))
    (sums,) = wait(cross_grad.state + outs[2:], sums, computed=(down_grad,))
    x_grad = outs[2].end().astype(F32)
    cross_grad = cross_grad.result()
    norm_mine = lax.dynamic_slice(sums, (0, lax.axis_index("dp") * rows), (8, rows)).T
    self_grad = self_grad.astype(F32)

    def piece(values, number):
        return values[:, number * heads_width : (number + 1) * heads_width]

    return (
        x_out,
        x_grad,
        source_grad,
        norm_mine[:, :3],
        norm_mine[:, 3:6],
        piece(self_grad, 0),
        piece(self_grad, 1),
        piece(self_grad, 2),
        jnp.concatenate(
            [cross_grad[:, two : two + heads_width // 2], cross_grad[:, -(heads_width // 2) :]], 1
        ),
        piece(cross_grad, 0),
        cross_grad[:, two + heads_width // 2 : two + 3 * heads_width // 2],
        cross_grad[:, two + 3 * heads_width // 2 : two + 5 * heads_width // 2],
        piece(cross_grad, 1),
        up_grad,
        down_grad,
    )


def solution(mesh):
    rows = P(AXES, None)
    split = P("dp", "tensor")
    narrow = P("dp", None)
    placed = (rows, rows, P(AXES), narrow, narrow, narrow) + (split,) * 10 + (rows,)
    return jax.shard_map(
        functools.partial(shards, Links(mesh.shape["dp"])),
        mesh=mesh,
        in_specs=placed,
        out_specs=(rows, rows, rows, narrow, narrow) + (split,) * 10,
        check_vma=False,
    )
```

```python
import functools

import jax
import jax.numpy as jnp
import numpy as np
from jax import lax
from jax.experimental import pallas as pl
from jax.experimental.pallas import tpu as pltpu
from jax.sharding import PartitionSpec as P

HEAD_DIM = 64
PAIR = 128
EPSILON = 1e-05
HIDDEN = -1e30
AXES = ("dp", "tensor")
BF = jnp.bfloat16
F32 = jnp.float32
VMEM_LIMIT = 50 * 2**20
KERNEL_COST = pl.CostEstimate(flops=1, bytes_accessed=1024, transcendentals=0)


def dot(former, latter, dims, kind=F32):
    return lax.dot_general(former, latter, (dims, ((), ())), preferred_element_type=kind)


def mm(former, latter, kind=F32):
    return dot(former, latter, ((1,), (0,)), kind)


def mm_lt(former, latter, kind=F32):
    return dot(former, latter, ((0,), (0,)), kind)


def mm_rt(former, latter, kind=F32):
    return dot(former, latter, ((1,), (1,)), kind)


def head_masks(values):
    lane = lax.broadcasted_iota(jnp.int32, values.shape, 1)
    zero = jnp.zeros_like(values)
    return (
        jnp.where(lane < HEAD_DIM, values, zero),
        jnp.where(lane >= HEAD_DIM, values, zero),
    )


def causal_bias(rows, columns, row_start, column_start):
    row = lax.broadcasted_iota(jnp.int32, (rows, columns), 0) + row_start
    column = lax.broadcasted_iota(jnp.int32, (rows, columns), 1) + column_start
    return row, column


def attention_kernel(tree, block, *refs):
    if tree:
        q_ref, k_ref, v_ref, qbits_ref, kbits_ref, o_ref, lse_ref, bias_ref = refs
    else:
        q_ref, k_ref, v_ref, o_ref, lse_ref = refs
    tokens = q_ref.shape[0]
    keys = k_ref.shape[0]
    half = tokens // 2
    if tree:

        @pl.when(pl.program_id(0) == 0)
        def _():
            row, column = causal_bias(half, half, 0, 0)
            seen = (qbits_ref[half:, :] & kbits_ref[:, half:]) != 0
            bias_ref[...] = jnp.where(seen & (column <= row), 0.0, HIDDEN)

    lane = lax.broadcasted_iota(jnp.int32, (block, PAIR), 1)
    for start in range(0, tokens, block):
        last = start + block if tree else keys
        queries = head_masks(q_ref[start : start + block, :] * BF(HEAD_DIM ** (-0.5)))
        key_rows = k_ref[:last, :]
        value_rows = v_ref[:last, :]
        outs = []
        sums = []
        for side in range(2):
            scores = mm_rt(queries[side], key_rows)
            if tree:
                if start < half:
                    row, column = causal_bias(block, block, 0, 0)
                    tail = scores[:, start:] + jnp.where(column <= row, 0.0, HIDDEN)
                    split = start
                else:
                    tail = (
                        scores[:, half:]
                        + bias_ref[start - half : start - half + block, : last - half]
                    )
                    split = half
                scores = tail if split == 0 else jnp.concatenate([scores[:, :split], tail], 1)
            top = jnp.max(scores, 1, keepdims=True)
            weights = jnp.exp(scores - top)
            total = jnp.sum(weights, 1, keepdims=True)
            outs.append(mm(weights.astype(BF), value_rows) * (1.0 / total))
            sums.append(top + jnp.log(total))
        o_ref[start : start + block, :] = jnp.where(lane < HEAD_DIM, outs[0], outs[1]).astype(BF)
        lse_ref[start : start + block, :] = jnp.where(lane < HEAD_DIM, sums[0], sums[1])


def attention(q, k, v, offsets, pairs, bits, block=512):
    tokens = q.shape[0]
    tree = bits is not None

    def spec(rows, shift):
        return pl.BlockSpec((rows, PAIR), lambda i, shift=shift: (0, i + shift))

    in_specs = [spec(tokens, offsets[0]), spec(k.shape[0], offsets[1]), spec(v.shape[0], offsets[2])]
    operands = [q, k, v]
    scratch = []
    if tree:
        in_specs += [
            pl.BlockSpec((tokens, 1), lambda i: (0, 0)),
            pl.BlockSpec((1, tokens), lambda i: (0, 0)),
        ]
        operands += list(bits)
        scratch = [pltpu.VMEM((tokens // 2, tokens // 2), F32)]
    return pl.pallas_call(
        functools.partial(attention_kernel, tree, block),
        grid=(pairs,),
        in_specs=in_specs,
        out_specs=[spec(tokens, 0), spec(tokens, 0)],
        out_shape=[
            jax.ShapeDtypeStruct((tokens, pairs * PAIR), BF),
            jax.ShapeDtypeStruct((tokens, pairs * PAIR), F32),
        ],
        scratch_shapes=scratch,
        compiler_params=pltpu.CompilerParams(vmem_limit_bytes=VMEM_LIMIT),
        cost_estimate=KERNEL_COST,
    )(*operands)


def attention_back_kernel(tree, block, *refs):
    if tree:
        (q_ref, k_ref, v_ref, o_ref, lse_ref, do_ref, qbits_ref, kbits_ref,
         dq_ref, dk_ref, dv_ref, dq_acc, bias_ref) = refs
    else:
        q_ref, k_ref, v_ref, o_ref, lse_ref, do_ref, dq_ref, dk_ref, dv_ref, dq_acc = refs
    tokens = q_ref.shape[0]
    keys = k_ref.shape[0]
    half = tokens // 2
    scale = HEAD_DIM ** (-0.5)
    if tree:

        @pl.when(pl.program_id(0) == 0)
        def _():
            row, column = causal_bias(half, half, 0, 0)
            seen = (kbits_ref[half:, :] & qbits_ref[:, half:]) != 0
            bias_ref[...] = jnp.where(seen & (row <= column), 0.0, HIDDEN)

    queries = head_masks(q_ref[...] * BF(scale))
    grads = head_masks(do_ref[...])
    pick_row = lax.broadcasted_iota(jnp.int32, (8, PAIR), 0)
    pick_lane = lax.broadcasted_iota(jnp.int32, (8, PAIR), 1)
    pick = ((pick_lane // HEAD_DIM) == pick_row).astype(F32)
    product = do_ref[...].astype(F32) * o_ref[...].astype(F32)
    delta = lax.dot_general(
        pick, product, (((1,), (1,)), ((), ())), precision=lax.Precision.HIGHEST,
        preferred_element_type=F32,
    )
    lse_rows = jnp.transpose(lse_ref[...])
    keys_across = jnp.transpose(k_ref[...].astype(F32)).astype(BF)
    row = lax.broadcasted_iota(jnp.int32, keys_across.shape, 0)
    zero = jnp.zeros_like(keys_across)
    keys_across = (
        jnp.where(row < HEAD_DIM, keys_across, zero),
        jnp.where(row >= HEAD_DIM, keys_across, zero),
    )
    for start in range(0, keys, block):
        first = start if tree else 0
        key_rows = k_ref[start : start + block, :]
        value_rows = v_ref[start : start + block, :]
        dv = None
        dk = None
        dq = None
        for side in range(2):
            stat = lse_rows[side * HEAD_DIM : side * HEAD_DIM + 1, first:]
            scores = mm_rt(key_rows, queries[side][first:, :]) - stat
            if tree:
                if start < half:
                    row, column = causal_bias(block, block, 0, 0)
                    head = scores[:, :block] + jnp.where(row <= column, 0.0, HIDDEN)
                    scores = jnp.concatenate([head, scores[:, block:]], 1)
                else:
                    scores = scores + bias_ref[start - half : start - half + block, first - half :]
            weights = jnp.exp(scores)
            dv_part = mm(weights.astype(BF), grads[side][first:, :])
            weight_grad = mm_rt(value_rows, grads[side][first:, :])
            score_grad = (weights * (weight_grad - delta[side : side + 1, first:])).astype(BF)
            dk_part = mm(score_grad, queries[side][first:, :])
            dq_part = mm(keys_across[side][:, start : start + block], score_grad)
            dv = dv_part if dv is None else dv + dv_part
            dk = dk_part if dk is None else dk + dk_part
            dq = dq_part if dq is None else dq + dq_part
        dv_ref[start : start + block, :] = dv.astype(BF)
        dk_ref[start : start + block, :] = dk.astype(BF)
        if start == 0:
            dq_acc[...] = dq
        else:
            dq_acc[:, first:] += dq
    dq_ref[...] = (jnp.transpose(dq_acc[...]) * scale).astype(BF)


def attention_back(q, k, v, o, lse, do, offsets, pairs, bits):
    tokens = q.shape[0]
    keys = k.shape[0]
    tree = bits is not None
    block = 256 if tree else 512

    def spec(rows, shift):
        return pl.BlockSpec((rows, PAIR), lambda i, shift=shift: (0, i + shift))

    in_specs = [
        spec(tokens, offsets[0]), spec(keys, offsets[1]), spec(keys, offsets[2]),
        spec(tokens, 0), spec(tokens, 0), spec(tokens, 0),
    ]
    operands = [q, k, v, o, lse, do]
    scratch = [pltpu.VMEM((PAIR, tokens), F32)]
    if tree:
        in_specs += [
            pl.BlockSpec((1, tokens), lambda i: (0, 0)),
            pl.BlockSpec((tokens, 1), lambda i: (0, 0)),
        ]
        operands += list(bits)
        scratch.append(pltpu.VMEM((tokens // 2, tokens // 2), F32))
    return pl.pallas_call(
        functools.partial(attention_back_kernel, tree, block),
        grid=(pairs,),
        in_specs=in_specs,
        out_specs=[spec(tokens, 0), spec(keys, 0), spec(keys, 0)],
        out_shape=[
            jax.ShapeDtypeStruct((tokens, pairs * PAIR), BF),
            jax.ShapeDtypeStruct((keys, pairs * PAIR), BF),
            jax.ShapeDtypeStruct((keys, pairs * PAIR), BF),
        ],
        scratch_shapes=scratch,
        compiler_params=pltpu.CompilerParams(vmem_limit_bytes=VMEM_LIMIT),
        cost_estimate=KERNEL_COST,
    )(*operands)


def pick(values, index, axis):
    return lax.dynamic_index_in_dim(values, index, axis, keepdims=False)


class Pending:
    def __init__(self, finish, *received):
        self.finish, self.received = finish, list(received)

    def end(self):
        return self.finish(*self.received)


def wait(pendings, *values, computed=()):
    marks = [lax.slice(v, (0,) * v.ndim, (1,) * (v.ndim - 2) + (8, PAIR)) for v in computed]
    received, values, _ = lax.optimization_barrier(([p.received for p in pendings], values, marks))
    for pending, got in zip(pendings, received):
        pending.received = got
    return values


class Links:
    def __init__(self, dp_size):
        self.devices = 2 * dp_size
        self.places = dp_size // 2
        self.grid = dp_size == 16

    def begin(self):
        self.place = lax.axis_index("dp") // 2
        self.core = lax.axis_index("dp") % 2
        self.side = lax.axis_index("tensor")
        self.home = self.core == self.side

    def send(self, values, pairs):
        return lax.ppermute(values, AXES, pairs)

    def flip(self, values, bit):
        return self.send(values, [(i, i ^ bit) for i in range(self.devices)])

    def quad(self, values, edges):
        pairs = [(4 * m + s, 4 * m + t) for m in range(self.places) for s, t in edges]
        return self.send(values, pairs)

    def cross(self, values):
        return Pending(
            lambda got: jnp.where(self.home, values, got), self.quad(values, [(1, 2), (2, 1)])
        )

    def swap_cores(self, values):
        return self.quad(values, [(0, 2), (1, 3), (2, 0), (3, 1)])

    def groups(self):
        return [[2 * m + c for m in range(self.places)] for c in range(2)]

    def gather(self, shard):
        return lax.all_gather(shard, "dp", axis=0, tiled=True)

    def sides(self, shard):
        def finish(near, far):
            near = jnp.where(self.home, shard, near)
            first = self.side == 0
            return jnp.concatenate([jnp.where(first, near, far), jnp.where(first, far, near)], 0)

        return Pending(
            finish,
            self.quad(shard, [(1, 2), (2, 1)]),
            self.quad(shard, [(0, 1), (1, 3), (3, 2), (2, 0)]),
        )

    def gather_places(self, both):
        return lax.all_gather(both, "dp", axis=0, tiled=True, axis_index_groups=self.groups())

    def scatter(self, grad):
        return lax.psum_scatter(grad, "dp", scatter_dimension=0, tiled=True)

    def scatter_places(self, grad):
        return lax.psum_scatter(
            grad, "dp", scatter_dimension=0, tiled=True, axis_index_groups=self.groups()
        )

    def sides_back(self, parts, axis):
        mine, other = (
            jnp.concatenate([pick(part, index, axis) for part in parts], -1)
            for index in (self.side, 1 - self.side)
        )
        return Pending(
            lambda near, far: jnp.where(self.home, mine, near).astype(F32) + far.astype(F32),
            self.quad(mine, [(1, 2), (2, 1)]),
            self.quad(other, [(1, 0), (3, 1), (2, 3), (0, 2)]),
        )

    def halve(self, parts, axis, bit, index):
        kept, sent = (
            jnp.concatenate([pick(part, i, axis) for part in parts], -1) for i in (index, 1 - index)
        )
        return Pending(
            lambda got: kept.astype(F32) + got.astype(F32), self.flip(sent, bit)
        )

    def total(self, values, bits):
        if not self.grid:
            return lax.psum(values, AXES) if 1 in bits else values
        for bit in bits:
            values = values + self.flip(values, bit)
        return values


class Scatter:
    def __init__(self, links, first, second):
        self.links = links
        if not links.grid:
            whole = links.scatter_places(jnp.concatenate(list(first) + list(second), 1))
            self.state = [links.sides_back([whole.reshape(2, -1, whole.shape[1])], 0)]
            return
        former, latter = (
            [part.reshape(2, 2, 2, 2, part.shape[0] // 16, part.shape[1]) for part in parts]
            for parts in (first, second)
        )
        self.state = [
            links.sides_back(former, 3), links.halve(latter, 2, 4, links.place % 2)
        ]

    def second(self):
        links = self.links
        if links.grid:
            former, latter = (pending.end().astype(BF) for pending in self.state)
            self.state = [
                links.halve([former], 2, 4, links.place % 2), links.sides_back([latter], 2)
            ]

    def far(self):
        links = self.links
        if links.grid:
            both = jnp.concatenate([pending.end().astype(BF) for pending in self.state], -1)
            self.state = [links.halve([both], 0, 16, links.place // 4)]

    def near(self):
        links = self.links
        if links.grid:
            whole = self.state[0].end().astype(BF)
            self.state = [links.halve([whole], 0, 8, links.place // 2 % 2)]

    def result(self):
        return self.state[0].end()


def ancestor_bits(segment_all, parent_row):
    nodes = parent_row.shape[0]
    node_ids = jnp.arange(nodes, dtype=jnp.int32)
    current = node_ids
    seen = jnp.zeros((nodes,), jnp.int32)
    for _ in range(nodes):
        seen = seen | jnp.left_shift(1, current)
        current = jnp.sum(jnp.where(current[:, None] == node_ids[None, :], parent_row[None, :], 0), 1)
    query_bits = jnp.sum(
        jnp.where(segment_all[:, None] == node_ids[None, :], seen[None, :], 0), 1
    )
    return query_bits, jnp.left_shift(1, segment_all)


def norm_stats(values):
    mean = jnp.mean(values, -1, keepdims=True)
    centered = values - mean
    variance = jnp.mean(centered * centered, -1, keepdims=True)
    return centered, lax.rsqrt(variance + EPSILON)


def norm(values, gain_row, offset):
    centered, inverse = norm_stats(values)
    return centered * inverse * gain_row + offset


def norm_back(values, gain_row, grad):
    centered, inverse = norm_stats(values)
    normed = centered * inverse
    scaled = grad * gain_row
    back = inverse * (
        scaled
        - jnp.mean(scaled, -1, keepdims=True)
        - normed * jnp.mean(scaled * normed, -1, keepdims=True)
    )
    return back, grad * normed


def shards(
    links,
    x_in,
    source,
    segment,
    parent,
    norm_gain,
    norm_bias,
    self_query,
    self_key,
    self_value,
    self_output,
    cross_query,
    cross_key,
    cross_value,
    cross_output,
    ffn_up,
    ffn_down,
    cotangent,
):
    half, width = x_in.shape
    tokens = 2 * half
    rows = self_query.shape[0]
    heads_width = self_query.shape[1]
    hidden = ffn_up.shape[1]
    pairs = heads_width // PAIR
    links.begin()
    first_core = links.core == 0

    def both_halves(mine):
        other = links.swap_cores(mine)
        return jnp.concatenate(
            [jnp.where(first_core, mine, other), jnp.where(first_core, other, mine)], 0
        )

    def my_half(values, first=first_core):
        return jnp.where(first, values[:half], values[half:])

    def other_half(values, first=first_core):
        return jnp.where(first, values[half:], values[:half])

    def joined(part):
        return part.astype(F32) + links.swap_cores(part).astype(F32)

    def joined_half(part, first=first_core):
        sent = links.swap_cores(other_half(part, first))
        return my_half(part, first).astype(F32) + sent.astype(F32)

    nodes = parent.shape[1]
    labels = jnp.concatenate(
        [segment, parent[0], jnp.zeros((PAIR - nodes,), jnp.int32)]
    ).reshape(-1, PAIR)
    segment_rows = half // PAIR
    pad = PAIR - norm_gain.shape[1] - norm_bias.shape[1]
    norms_shard = jnp.concatenate(
        [norm_gain, norm_bias, jnp.zeros((rows, pad), BF)], 1
    )
    two, three, four = 2 * heads_width, 3 * heads_width, 4 * heads_width
    self_w = links.gather(
        jnp.concatenate([self_query, self_key, self_value, self_output, norms_shard], 1)
    )
    cross_w = links.gather(
        jnp.concatenate([cross_query, cross_key, cross_value, cross_output], 1)
    )
    up_w = links.gather(ffn_up)
    moved = [links.cross(x_in), links.cross(labels), links.cross(jnp.concatenate([source, cotangent], 0))]
    down_w = links.sides(ffn_down)
    whole = Pending(lambda got: got, self_w)
    wait(moved + [down_w, whole])
    self_w = links.cross(whole.end())
    down_w = links.gather_places(down_w.end())
    x_mine, labels, others = (pending.end() for pending in moved)
    x_zero = both_halves(x_mine).astype(F32)
    segment_all = both_halves(labels[:segment_rows]).reshape(tokens)
    query_bits, key_bits = ancestor_bits(segment_all, labels[segment_rows, :nodes])
    forward_bits = (query_bits[:, None], key_bits[None, :])
    backward_bits = (query_bits[None, :], key_bits[:, None])
    source_all = both_halves(others[:half])
    grad_top = both_halves(others[half:])
    centered, inverse = norm_stats(x_zero)
    normed = centered * inverse
    whole = Pending(lambda got: got, cross_w)
    wait([self_w, whole], computed=(normed, source_all, grad_top))
    cross_w = links.cross(whole.end())
    self_w = self_w.end()
    norms = self_w[:, four : four + 8].astype(F32).T
    gain = [norms[i : i + 1] for i in range(3)]
    shift = [norms[i + 3 : i + 4] for i in range(3)]

    hidden_one = (normed * gain[0] + shift[0]).astype(BF)
    qkv = mm(hidden_one, self_w[:, :three], BF)
    self_places = (0, pairs, 2 * pairs)
    mixed_one, lse_one = attention(qkv, qkv, qkv, self_places, pairs, forward_bits)
    x_one = x_zero + joined(mm_rt(mixed_one, self_w[:, three:four], BF))
    hidden_two = norm(x_one, gain[1], shift[1]).astype(BF)
    whole = Pending(lambda got: got, up_w)
    (hidden_two,) = wait([whole], hidden_two)
    up_w = links.cross(whole.end())
    cross_w = cross_w.end()
    cross_queries = mm(hidden_two, cross_w[:, :heads_width], BF)
    memory = mm(source_all, cross_w[:, heads_width:three], BF)
    cross_places = (0, 0, pairs)
    mixed_two, lse_two = attention(cross_queries, memory, memory, cross_places, pairs, None)
    x_two = x_one + joined(mm_rt(mixed_two, cross_w[:, three:four], BF))
    hidden_three = norm(x_two, gain[2], shift[2]).astype(BF)
    (hidden_three,) = wait([up_w], hidden_three)
    up_w = up_w.end()
    active = mm(hidden_three, up_w)
    normal = 0.5 * (1.0 + lax.erf(active * np.float32(0.5**0.5)))
    slope = (
        normal + active * jnp.exp(-0.5 * active * active) * np.float32((2.0 * np.pi) ** -0.5)
    ).astype(BF)
    activated = (active * normal).astype(BF)
    down_grad = mm_lt(grad_top, activated, BF)
    whole = Pending(lambda got: got, down_w)
    down_grad, activated, slope = wait([whole], down_grad, activated, slope)
    down_w = whole.end()

    def norm_sums(values, grad):
        return jnp.sum(my_half(values), 0), jnp.sum(my_half(grad), 0)

    down_grad = links.scatter_places(down_grad)
    active_grad = (mm(grad_top, down_w) * slope.astype(F32)).astype(BF)
    up_grad = links.cross(mm_lt(hidden_three, active_grad, BF))
    normed_grad = joined(mm_rt(active_grad, up_w, BF))
    back, gain_part = norm_back(x_two, gain[2], normed_grad)
    gain_three, shift_three = norm_sums(gain_part, normed_grad)
    grad_two = grad_top.astype(F32) + back
    grad_two_low = grad_two.astype(BF)
    mixed_grad = mm(grad_two_low, cross_w[:, three:four], BF)
    dq, dk, dv = attention_back(
        cross_queries, memory, memory, mixed_two, lse_two, mixed_grad, cross_places, pairs, None
    )
    down_grad = Pending(lambda got: got, down_grad)
    part = mm_rt(dq, cross_w[:, :heads_width], BF)
    dkv = jnp.concatenate([dk, dv], 1)
    cross_q_grad = mm_lt(hidden_two, dq, BF)
    cross_o_grad = mm_lt(grad_two_low, mixed_two, BF)
    cross_kv_grad = mm_lt(source_all, dkv, BF)
    normed_grad = joined(part)
    (gain_row,) = wait([up_grad, down_grad], gain[1], computed=(part, cross_q_grad, cross_o_grad))
    up_grad, gain_row = wait([], up_grad.end(), gain_row)
    up_grad = Pending(lambda got: got, links.scatter(up_grad))
    back, gain_part = norm_back(x_one, gain_row, normed_grad)
    gain_two, shift_two = norm_sums(gain_part, normed_grad)
    grad_one = grad_two + back
    grad_one_low = grad_one.astype(BF)
    self_o_grad = mm_lt(grad_one_low, mixed_one, BF)
    cross_grad = Scatter(
        links,
        [cross_q_grad, cross_o_grad, self_o_grad[:, : heads_width // 2]],
        [cross_kv_grad, self_o_grad[:, heads_width // 2 :]],
    )
    mixed_grad = mm(grad_one_low, self_w[:, three:four], BF)
    dq, dk, dv = attention_back(
        qkv, qkv, qkv, mixed_one, lse_one, mixed_grad, self_places, pairs, backward_bits
    )
    dqkv = jnp.concatenate([dq, dk, dv], 1)
    qkv_grad = mm_lt(hidden_one, dqkv, BF)
    self_grad = links.cross(qkv_grad)
    part = mm_rt(dqkv, self_w[:, :three], BF)
    part, down_late, cross_late = wait(
        cross_grad.state, part, down_w, cross_w, computed=(qkv_grad,)
    )
    cross_grad.second()
    normed_grad = joined_half(part)
    out_part = mm_rt(activated, down_late, BF)
    source_part = mm_rt(dkv, cross_late[:, heads_width:three], BF)
    wait([self_grad], computed=(out_part, source_part))
    self_grad, first_late, gain_zero = wait([], self_grad.end(), first_core, gain[0])
    self_grad = links.scatter(self_grad)
    x_three = (my_half(x_two, first_late) + joined_half(out_part, first_late)).astype(BF)
    source_part = joined_half(source_part, first_late).astype(BF)
    outs = [links.cross(v) for v in (x_three, source_part)]
    (gain_zero,) = wait(cross_grad.state, gain_zero)
    cross_grad.far()
    back, gain_part = norm_back(my_half(x_zero), gain_zero, normed_grad)
    gain_one, shift_one = jnp.sum(gain_part, 0), jnp.sum(normed_grad, 0)
    x_grad_mine = (my_half(grad_one) + back).astype(BF)
    sums = jnp.stack(
        [gain_one, gain_two, gain_three, shift_one, shift_two, shift_three,
         jnp.zeros_like(gain_one), jnp.zeros_like(gain_one)]
    )
    (sums,) = wait(outs, sums, computed=(x_grad_mine,))
    outs.append(links.cross(x_grad_mine))
    down_grad = links.sides_back([down_grad.end().reshape(2, -1, hidden)], 0)
    x_out, source_grad = (pending.end() for pending in outs[:2])
    source_grad = source_grad.astype(F32)
    up_grad = up_grad.end().astype(F32)
    sums = links.total(sums, (2, 4))
    (sums,) = wait(cross_grad.state + [down_grad], sums, computed=(source_grad, up_grad))
    cross_grad.near()
    down_grad = down_grad.end()
    sums = links.total(sums, (8, 16, 1))
    (sums,) = wait(cross_grad.state + outs[2:], sums, computed=(down_grad,))
    x_grad = outs[2].end().astype(F32)
    cross_grad = cross_grad.result()
    norm_mine = lax.dynamic_slice(sums, (0, lax.axis_index("dp") * rows), (8, rows)).T
    self_grad = self_grad.astype(F32)

    def piece(values, number):
        return values[:, number * heads_width : (number + 1) * heads_width]

    return (
        x_out,
        x_grad,
        source_grad,
        norm_mine[:, :3],
        norm_mine[:, 3:6],
        piece(self_grad, 0),
        piece(self_grad, 1),
        piece(self_grad, 2),
        jnp.concatenate(
            [cross_grad[:, two : two + heads_width // 2], cross_grad[:, -(heads_width // 2) :]], 1
        ),
        piece(cross_grad, 0),
        cross_grad[:, two + heads_width // 2 : two + 3 * heads_width // 2],
        cross_grad[:, two + 3 * heads_width // 2 : two + 5 * heads_width // 2],
        piece(cross_grad, 1),
        up_grad,
        down_grad,
    )


def solution(mesh):
    rows = P(AXES, None)
    split = P("dp", "tensor")
    narrow = P("dp", None)
    placed = (rows, rows, P(AXES), narrow, narrow, narrow) + (split,) * 10 + (rows,)
    return jax.shard_map(
        functools.partial(shards, Links(mesh.shape["dp"])),
        mesh=mesh,
        in_specs=placed,
        out_specs=(rows, rows, rows, narrow, narrow) + (split,) * 10,
        check_vma=False,
    )
```
